512 devices in a mesh: dp: 2 (over y_hi), row: 16 (over z, core), col: 16 (over y_lo, x).
Axes of the slice: x: 4, y: 8 (y_hi: 2, y_lo: 4; y = y_hi * 4 + y_lo), z: 8, core: 2. Of those that a mesh axis runs over, the one named last changes fastest.
Arguments:
- features: bfloat16 [4096, 3072], P(('dp', 'row'), 'col'), may hold values from -6 to 6
- up_weight: bfloat16 [3072, 24576], P('row', 'col'), may hold values from -0.109375 to 0.109375
- out_grad: bfloat16 [4096, 24576], P(('dp', 'row'), 'col'), may hold values from -6 to 6
Outputs:
- gelu_out: bfloat16 [4096, 24576], P(('dp', 'row'), 'col')
- feature_grad: bfloat16 [4096, 3072], P(('dp', 'row'), 'col')
- weight_grad: float32 [3072, 24576], P('row', 'col')
The draws below stay inside these ranges and needn't reach their ends.
All inputs are finite; a program needn't handle non-finite values.
Results may differ from the reference program's by a relative error of at most 0.022.
Values may be sent and summed in bfloat16 or wider, within the bound.
No kernel may reach another device: no remote copies, remote signals or barrier semaphores. Data moves between devices by JAX's collectives and lax.ppermute only.
A program may use at most 64 MiB of HBM per device.

```python
import math
import jax
import jax.numpy as jnp
from jax import lax

D = 3072
FF = 24576
TOKENS = 4096
HID_TILE = 1536
N_COL = 16


def levels(key, shape, pieces, least, high):
    def one(position, parts):
        draws = jax.random.uniform(jax.random.fold_in(jax.random.fold_in(key, 6), position), (parts,), jnp.float32, least / len(pieces), high / len(pieces))
        return jnp.repeat(jnp.exp(draws), shape[position] // parts).reshape((-1,) + (1,) * (len(shape) - position - 1))

    factor_of = one(*pieces[0])
    for cut in pieces[1:]:
        factor_of = factor_of * one(*cut)
    return factor_of


def gaussian(rng, extent, width, most, cuts=(), held_as=jnp.bfloat16):
    result = width * jax.random.normal(rng, extent, jnp.float32)
    if cuts:
        result = result * levels(rng, extent, cuts, -0.22, 0.18)
    return jnp.clip(result, -most, most).astype(held_as)


def setup_inputs(seed: int = 0) -> dict:
    streams_of = jax.random.split(jax.random.key(seed), 4)
    features = gaussian(streams_of[0], (TOKENS, D), 1.0, 6.0, ((0, 32), (1, 16)))
    up_weight = gaussian(streams_of[1], (D, FF), D ** -0.5, 0.109375, ((0, 16), (1, 16)))
    out_grad = gaussian(streams_of[2], (TOKENS, FF), 1.0, 6.0, ((0, 32), (1, 16)))
    return {"features": features, "up_weight": up_weight, "out_grad": out_grad}


def reference(features, up_weight, out_grad):
    hidden = jnp.dot(features, up_weight, preferred_element_type=jnp.float32)
    normal_cdf = 0.5 * (1.0 + jax.scipy.special.erf(hidden / math.sqrt(2.0)))
    density = jnp.exp(-0.5 * hidden * hidden) / math.sqrt(2.0 * math.pi)
    gelu_out = (hidden * normal_cdf).astype(jnp.bfloat16)
    hidden_grad = (out_grad.astype(jnp.float32) * (normal_cdf + hidden * density)).astype(jnp.bfloat16)
    grad_blocks = jnp.moveaxis(hidden_grad.reshape(TOKENS, N_COL, HID_TILE), 1, 0)
    weight_blocks = jnp.moveaxis(up_weight.reshape(D, N_COL, HID_TILE), 1, 0)

    def add_block(running, pair):
        grad_block, weight_block = pair
        term = jnp.dot(grad_block, weight_block.T, preferred_element_type=jnp.float32)
        return (running + term.astype(jnp.bfloat16).astype(jnp.float32), None)
    start = jnp.zeros((TOKENS, D), jnp.float32)
    summed, _ = lax.scan(add_block, start, (grad_blocks, weight_blocks))
    feature_grad = summed.astype(jnp.bfloat16)
    weight_grad = jnp.dot(features.T, hidden_grad, preferred_element_type=jnp.float32)
    return (gelu_out, feature_grad, weight_grad)
```

```python
import math

import jax
import jax.numpy as jnp
from jax import lax
from jax.sharding import PartitionSpec as P

ROWS = 16


def per_device(features, up_weight, out_grad):
    tokens, depth = features.shape
    weight = lax.all_gather(up_weight, "row", axis=0, tiled=True)
    token_rows = lax.all_gather(features, "col", axis=1, tiled=True)
    swap = [(r * ROWS + c, c * ROWS + r) for r in range(ROWS) for c in range(ROWS)]
    turned = lax.ppermute(features, ("row", "col"), swap)
    column = lax.all_gather(turned, "col", axis=0, tiled=True)

    hidden = jnp.dot(token_rows, weight, preferred_element_type=jnp.float32)
    normal_cdf = 0.5 * (1.0 + jax.scipy.special.erf(hidden / math.sqrt(2.0)))
    density = jnp.exp(-0.5 * hidden * hidden) / math.sqrt(2.0 * math.pi)
    gelu_out = (hidden * normal_cdf).astype(jnp.bfloat16)
    hidden_grad = (out_grad.astype(jnp.float32) * (normal_cdf + hidden * density)).astype(
        jnp.bfloat16
    )
    grad_cols = lax.all_gather(hidden_grad, "row", axis=0, tiled=True)

    contract_last = (((1,), (1,)), ((), ()))
    partial_value = lax.dot_general(
        weight, hidden_grad, contract_last, preferred_element_type=jnp.float32
    ).astype(jnp.bfloat16)
    pieces = lax.all_to_all(
        partial_value.reshape(ROWS, depth, tokens), "col", 0, 0, tiled=True
    )
    feature_grad = jnp.sum(pieces.astype(jnp.float32), axis=0).astype(jnp.bfloat16).T

    grad_cols, feature_grad = lax.optimization_barrier((grad_cols, feature_grad))
    own_grad = lax.dot_general(
        column, grad_cols, (((0,), (0,)), ((), ())), preferred_element_type=jnp.float32
    ).astype(jnp.bfloat16)
    other_grad = lax.ppermute(own_grad, "dp", [(0, 1), (1, 0)])
    weight_grad = own_grad.astype(jnp.float32) + other_grad.astype(jnp.float32)
    return (gelu_out, feature_grad, weight_grad)


def solution(mesh):
    placed = (P(("dp", "row"), "col"), P("row", "col"), P(("dp", "row"), "col"))
    return jax.shard_map(
        per_device,
        mesh=mesh,
        in_specs=placed,
        out_specs=(P(("dp", "row"), "col"), P(("dp", "row"), "col"), P("row", "col")),
        check_vma=False,
    )
```

```python
import math

import jax
import jax.numpy as jnp
from jax import lax
from jax.sharding import PartitionSpec as P

ROWS = 16
COLS = 16
CHIPS = ROWS // 2
ROUNDS = CHIPS // 2
SLOTS = CHIPS
PARTS = 2


def held_from(chip, core, slot):
    steps = (slot + 1) // 2
    parity = core if slot % 2 or slot == 0 else 1 - core
    away = -steps if core == 0 else steps
    return 2 * ((chip + away) % CHIPS) + parity


def every_place():
    for chip in range(CHIPS):
        for core in range(2):
            for slot in range(SLOTS):
                for other in range(2):
                    yield chip, core, slot, other


def depth_moves():
    return [
        (
            (2 * chip + (core ^ other)) * COLS + held_from(chip, core, slot),
            (2 * chip + core) * COLS + 2 * slot + other,
        )
        for chip, core, slot, other in every_place()
    ]


def token_moves():
    return [
        (
            held_from(chip, core, slot) * COLS + 2 * chip + (core ^ other),
            (2 * chip + core) * COLS + 2 * slot + other,
        )
        for chip, core, slot, other in every_place()
    ]


def ring_moves(cross):
    moves = []
    for chip in range(CHIPS):
        moves.append((2 * chip + cross, 2 * ((chip + 1) % CHIPS)))
        moves.append((2 * chip + 1 - cross, 2 * ((chip - 1) % CHIPS) + 1))
    return moves


def ring(block):
    slots = [block]
    same = cross = block
    for step in range(1, ROUNDS + 1):
        same = lax.ppermute(same, "row", ring_moves(0))
        slots.append(same)
        if step < ROUNDS:
            cross = lax.ppermute(cross, "row", ring_moves(1 if step == 1 else 0))
            slots.append(cross)
    return slots


def to_other_core(value):
    return lax.ppermute(value, "row", [(row, row ^ 1) for row in range(ROWS)])


def to_all_cols(block):
    copies = jnp.broadcast_to(block[None], (COLS,) + block.shape)
    return lax.all_to_all(copies, "col", 0, 0, tiled=True)


def per_device(features, up_weight, out_grad):
    tokens, depth = features.shape
    hidden_units = up_weight.shape[1]
    features = features.T
    weights = ring(up_weight)
    by_depth = to_all_cols(lax.ppermute(features, ("row", "col"), depth_moves()))
    by_token = to_all_cols(lax.ppermute(features, ("row", "col"), token_moves()))

    both = 0.0
    for slot, weight in enumerate(weights):
        block = jnp.concatenate([by_depth[2 * slot], by_depth[2 * slot + 1]], axis=1)
        both += lax.dot_general(
            block, weight, (((0,), (0,)), ((), ())), preferred_element_type=jnp.float32
        )
    hidden = both[:tokens] + to_other_core(both[tokens:].astype(jnp.bfloat16)).astype(jnp.float32)
    normal_cdf = 0.5 * (1.0 + jax.scipy.special.erf(hidden / math.sqrt(2.0)))
    density = jnp.exp(-0.5 * hidden * hidden) / math.sqrt(2.0 * math.pi)
    gelu_out = (hidden * normal_cdf).astype(jnp.bfloat16)
    hidden_grad = (out_grad.astype(jnp.float32) * (normal_cdf + hidden * density)).astype(
        jnp.bfloat16
    )

    width = hidden_units // PARTS
    totals = []
    for part in range(PARTS):
        total = 0.0
        for slot, grad in enumerate(ring(hidden_grad[:, part * width : (part + 1) * width])):
            block = by_token[2 * slot : 2 * slot + 2].reshape(2 * depth, tokens)
            total += jnp.dot(block, grad, preferred_element_type=jnp.float32)
        totals.append(total)

    chip_grad = jnp.concatenate([hidden_grad, to_other_core(hidden_grad)], axis=0)
    pieces = []
    for weight in weights:
        piece = lax.dot_general(
            weight, chip_grad, (((1,), (1,)), ((), ())), preferred_element_type=jnp.float32
        ).astype(jnp.bfloat16)
        pieces += [piece[:, :tokens], piece[:, tokens:]]
    pieces = lax.all_to_all(jnp.stack(pieces), "col", 0, 0, tiled=True)
    feature_grad = jnp.sum(pieces.astype(jnp.float32), axis=0).astype(jnp.bfloat16)
    feature_grad = lax.ppermute(
        feature_grad, ("row", "col"), [(to, source) for source, to in depth_moves()]
    ).T

    weight_grad = []
    for total in totals:
        own = total[:depth] + to_other_core(total[depth:].astype(jnp.bfloat16)).astype(jnp.float32)
        own = own.astype(jnp.bfloat16)
        replica = lax.ppermute(own, "dp", [(0, 1), (1, 0)])
        weight_grad.append(own.astype(jnp.float32) + replica.astype(jnp.float32))
    return (gelu_out, feature_grad, jnp.concatenate(weight_grad, axis=1))


def solution(mesh):
    placed = (P(("dp", "row"), "col"), P("row", "col"), P(("dp", "row"), "col"))
    return jax.shard_map(
        per_device,
        mesh=mesh,
        in_specs=placed,
        out_specs=(P(("dp", "row"), "col"), P(("dp", "row"), "col"), P("row", "col")),
        check_vma=False,
    )
```

```python
import math

import jax
import jax.numpy as jnp
from jax import lax
from jax.experimental import pallas as pl
from jax.experimental.pallas import tpu as pltpu
from jax.sharding import PartitionSpec as P

ROWS = 16
COLS = 16
CHIPS = ROWS // 2
ROUNDS = CHIPS // 2
SLOTS = CHIPS
PARTS = 2


def held_from(chip, core, slot):
    steps = (slot + 1) // 2
    parity = core if slot % 2 or slot == 0 else 1 - core
    away = -steps if core == 0 else steps
    return 2 * ((chip + away) % CHIPS) + parity


def every_place():
    for chip in range(CHIPS):
        for core in range(2):
            for slot in range(SLOTS):
                for other in range(2):
                    yield chip, core, slot, other


def depth_moves():
    return [
        (
            (2 * chip + (core ^ other)) * COLS + held_from(chip, core, slot),
            (2 * chip + core) * COLS + 2 * slot + other,
        )
        for chip, core, slot, other in every_place()
    ]


def token_moves():
    return [
        (
            held_from(chip, core, slot) * COLS + 2 * chip + (core ^ other),
            (2 * chip + core) * COLS + 2 * slot + other,
        )
        for chip, core, slot, other in every_place()
    ]


def ring_moves(cross):
    moves = []
    for chip in range(CHIPS):
        moves.append((2 * chip + cross, 2 * ((chip + 1) % CHIPS)))
        moves.append((2 * chip + 1 - cross, 2 * ((chip - 1) % CHIPS) + 1))
    return moves


def ring(block):
    slots = [block]
    same = cross = block
    for step in range(1, ROUNDS + 1):
        same = lax.ppermute(same, "row", ring_moves(0))
        slots.append(same)
        if step < ROUNDS:
            cross = lax.ppermute(cross, "row", ring_moves(1 if step == 1 else 0))
            slots.append(cross)
    return slots


def to_other_core(value):
    return lax.ppermute(value, "row", [(row, row ^ 1) for row in range(ROWS)])


def to_all_cols(block):
    copies = jnp.broadcast_to(block[None], (COLS,) + block.shape)
    return lax.all_to_all(copies, "col", 0, 0, tiled=True)


def after(value, *others):
    return lax.optimization_barrier((value,) + others)[0]


def input_grad_kernel(grad_ref, *refs):
    *weight_refs, pieces_ref = refs
    tokens = pieces_ref.shape[2]
    for slot, weight_ref in enumerate(weight_refs):
        piece = lax.dot_general(
            weight_ref[...],
            grad_ref[...],
            (((1,), (1,)), ((), ())),
            preferred_element_type=jnp.float32,
        ).astype(jnp.bfloat16)
        pieces_ref[2 * slot] = piece[:, :tokens]
        pieces_ref[2 * slot + 1] = piece[:, tokens:]


def input_grad_pieces(chip_grad, weights):
    depth, hidden_units = weights[0].shape
    tokens = chip_grad.shape[0] // 2
    moved = (SLOTS * depth * hidden_units + chip_grad.size + SLOTS * depth * 2 * tokens) * 2
    return pl.pallas_call(
        input_grad_kernel,
        out_shape=jax.ShapeDtypeStruct((2 * SLOTS, depth, tokens), jnp.bfloat16),
        in_specs=[pl.BlockSpec(memory_space=pltpu.VMEM)] * (1 + SLOTS),
        out_specs=pl.BlockSpec(memory_space=pltpu.VMEM),
        compiler_params=pltpu.CompilerParams(vmem_limit_bytes=16 * 2**20),
        cost_estimate=pl.CostEstimate(
            flops=4 * SLOTS * depth * hidden_units * tokens,
            bytes_accessed=moved,
            transcendentals=0,
        ),
    )(chip_grad, *weights)


def per_device(features, up_weight, out_grad):
    tokens, depth = features.shape
    hidden_units = up_weight.shape[1]
    features = features.T
    weights = ring(up_weight)
    by_depth = lax.ppermute(features, ("row", "col"), depth_moves())
    by_token = lax.ppermute(features, ("row", "col"), token_moves())
    by_depth = to_all_cols(after(by_depth, weights[1]))
    by_token = to_all_cols(after(by_token, weights[3], by_depth))

    both = 0.0
    for slot, weight in enumerate(weights):
        block = jnp.concatenate([by_depth[2 * slot], by_depth[2 * slot + 1]], axis=1)
        both += lax.dot_general(
            block, weight, (((0,), (0,)), ((), ())), preferred_element_type=jnp.float32
        )
    both = after(both, by_token)
    hidden = both[:tokens] + to_other_core(both[tokens:].astype(jnp.bfloat16)).astype(jnp.float32)
    normal_cdf = 0.5 * (1.0 + jax.scipy.special.erf(hidden / math.sqrt(2.0)))
    density = jnp.exp(-0.5 * hidden * hidden) / math.sqrt(2.0 * math.pi)
    gelu_out = (hidden * normal_cdf).astype(jnp.bfloat16)
    hidden_grad = (out_grad.astype(jnp.float32) * (normal_cdf + hidden * density)).astype(
        jnp.bfloat16
    )

    chip_grad = jnp.concatenate([hidden_grad, to_other_core(hidden_grad)], axis=0)
    pieces = input_grad_pieces(chip_grad, weights)
    pieces = lax.all_to_all(pieces, "col", 0, 0, tiled=True)
    feature_grad = jnp.sum(pieces.astype(jnp.float32), axis=0).astype(jnp.bfloat16)
    feature_grad = lax.ppermute(
        feature_grad, ("row", "col"), [(to, source) for source, to in depth_moves()]
    )

    total = 0.0
    for slot, grad in enumerate(ring(hidden_grad)):
        block = by_token[2 * slot : 2 * slot + 2].reshape(2 * depth, tokens)
        total += jnp.dot(block, grad, preferred_element_type=jnp.float32)
    total = after(total, pieces)
    width = hidden_units // PARTS
    weight_grad = []
    for part in range(PARTS):
        share = total[:, part * width : (part + 1) * width]
        own = share[:depth] + to_other_core(share[depth:].astype(jnp.bfloat16)).astype(jnp.float32)
        own = after(own.astype(jnp.bfloat16), feature_grad)
        replica = lax.ppermute(own, "dp", [(0, 1), (1, 0)])
        weight_grad.append(own.astype(jnp.float32) + replica.astype(jnp.float32))
    feature_grad = feature_grad.T
    return (gelu_out, feature_grad, jnp.concatenate(weight_grad, axis=1))


def solution(mesh):
    placed = (P(("dp", "row"), "col"), P("row", "col"), P(("dp", "row"), "col"))
    return jax.shard_map(
        per_device,
        mesh=mesh,
        in_specs=placed,
        out_specs=(P(("dp", "row"), "col"), P(("dp", "row"), "col"), P("row", "col")),
        check_vma=False,
    )
```

```python
import math

import jax
import jax.numpy as jnp
from jax import lax
from jax.experimental import pallas as pl
from jax.experimental.pallas import tpu as pltpu
from jax.sharding import PartitionSpec as P

ROWS = 16
COLS = 16
CHIPS = ROWS // 2
ROUNDS = CHIPS // 2
SLOTS = CHIPS


def held_from(chip, core, slot):
    steps = (slot + 1) // 2
    parity = core if slot % 2 or slot == 0 else 1 - core
    away = -steps if core == 0 else steps
    return 2 * ((chip + away) % CHIPS) + parity


def every_place():
    for chip in range(CHIPS):
        for core in range(2):
            for slot in range(SLOTS):
                for other in range(2):
                    yield chip, core, slot, other


def depth_moves():
    return [
        (
            (2 * chip + (core ^ other)) * COLS + held_from(chip, core, slot),
            (2 * chip + core) * COLS + 2 * slot + other,
        )
        for chip, core, slot, other in every_place()
    ]


def token_moves():
    return [
        (
            held_from(chip, core, slot) * COLS + 2 * chip + (core ^ other),
            (2 * chip + core) * COLS + 2 * slot + other,
        )
        for chip, core, slot, other in every_place()
    ]


def ring_moves(cross):
    moves = []
    for chip in range(CHIPS):
        moves.append((2 * chip + cross, 2 * ((chip + 1) % CHIPS)))
        moves.append((2 * chip + 1 - cross, 2 * ((chip - 1) % CHIPS) + 1))
    return moves


def ring(block):
    slots = [block]
    same = cross = block
    for step in range(1, ROUNDS + 1):
        if step == ROUNDS:
            same = after(same, cross)
        same = lax.ppermute(same, "row", ring_moves(0))
        slots.append(same)
        if step < ROUNDS:
            cross = lax.ppermute(cross, "row", ring_moves(1 if step == 1 else 0))
            slots.append(cross)
    return slots


def to_other_core(value):
    return lax.ppermute(value, "row", [(row, row ^ 1) for row in range(ROWS)])


def to_all_cols(block):
    copies = jnp.broadcast_to(block[None], (COLS,) + block.shape)
    return lax.all_to_all(copies, "col", 0, 0, tiled=True)


def after(value, *others):
    return lax.optimization_barrier((value,) + others)[0]


def input_grad_kernel(grad_ref, *refs):
    *weight_refs, pieces_ref = refs
    tokens = pieces_ref.shape[2]
    for slot, weight_ref in enumerate(weight_refs):
        piece = lax.dot_general(
            weight_ref[...],
            grad_ref[...],
            (((1,), (1,)), ((), ())),
            preferred_element_type=jnp.float32,
        ).astype(jnp.bfloat16)
        pieces_ref[2 * slot] = piece[:, :tokens]
        pieces_ref[2 * slot + 1] = piece[:, tokens:]


def input_grad_pieces(chip_grad, weights):
    depth, hidden_units = weights[0].shape
    tokens = chip_grad.shape[0] // 2
    moved = (SLOTS * depth * hidden_units + chip_grad.size + SLOTS * depth * 2 * tokens) * 2
    return pl.pallas_call(
        input_grad_kernel,
        out_shape=jax.ShapeDtypeStruct((2 * SLOTS, depth, tokens), jnp.bfloat16),
        in_specs=[pl.BlockSpec(memory_space=pltpu.VMEM)] * (1 + SLOTS),
        out_specs=pl.BlockSpec(memory_space=pltpu.VMEM),
        compiler_params=pltpu.CompilerParams(vmem_limit_bytes=16 * 2**20),
        cost_estimate=pl.CostEstimate(
            flops=4 * SLOTS * depth * hidden_units * tokens,
            bytes_accessed=moved,
            transcendentals=0,
        ),
    )(chip_grad, *weights)


def per_device(features, up_weight, out_grad):
    tokens, depth = features.shape
    hidden_units = up_weight.shape[1]
    features = features.T
    weights = ring(up_weight)
    by_depth = lax.ppermute(features, ("row", "col"), depth_moves())
    by_token = lax.ppermute(features, ("row", "col"), token_moves())
    by_depth = to_all_cols(by_depth)
    by_token = to_all_cols(after(by_token, by_depth))

    both = 0.0
    for slot, weight in enumerate(weights):
        block = jnp.concatenate([by_depth[2 * slot], by_depth[2 * slot + 1]], axis=1)
        both += lax.dot_general(
            block, weight, (((0,), (0,)), ((), ())), preferred_element_type=jnp.float32
        )
    hidden = both[:tokens] + to_other_core(both[tokens:].astype(jnp.bfloat16)).astype(jnp.float32)
    normal_cdf = 0.5 * (1.0 + jax.scipy.special.erf(hidden / math.sqrt(2.0)))
    density = jnp.exp(-0.5 * hidden * hidden) / math.sqrt(2.0 * math.pi)
    gelu_out = (hidden * normal_cdf).astype(jnp.bfloat16)
    hidden_grad = (out_grad.astype(jnp.float32) * (normal_cdf + hidden * density)).astype(
        jnp.bfloat16
    )

    grads = ring(hidden_grad)
    chip_grad = jnp.concatenate([hidden_grad, to_other_core(hidden_grad)], axis=0)
    pieces = input_grad_pieces(after(chip_grad, grads[1], grads[2]), weights)
    pieces = lax.all_to_all(pieces, "col", 0, 0, tiled=True)
    feature_grad = jnp.sum(pieces.astype(jnp.float32), axis=0).astype(jnp.bfloat16)
    feature_grad = lax.ppermute(
        feature_grad, ("row", "col"), [(to, source) for source, to in depth_moves()]
    )

    total = 0.0
    for slot, grad in enumerate(grads):
        block = by_token[2 * slot : 2 * slot + 2].reshape(2 * depth, tokens)
        total += jnp.dot(block, grad, preferred_element_type=jnp.float32)
    total = after(total, feature_grad)
    own = total[:depth] + to_other_core(total[depth:].astype(jnp.bfloat16)).astype(jnp.float32)
    own = own.astype(jnp.bfloat16)
    replica = lax.ppermute(own, "dp", [(0, 1), (1, 0)])
    weight_grad = own.astype(jnp.float32) + replica.astype(jnp.float32)
    feature_grad = feature_grad.T
    return (gelu_out, feature_grad, weight_grad)


def solution(mesh):
    placed = (P(("dp", "row"), "col"), P("row", "col"), P(("dp", "row"), "col"))
    return jax.shard_map(
        per_device,
        mesh=mesh,
        in_specs=placed,
        out_specs=(P(("dp", "row"), "col"), P(("dp", "row"), "col"), P("row", "col")),
        check_vma=False,
    )
```

```python
import functools
import math

import jax
import jax.numpy as jnp
from jax import lax
from jax.experimental import pallas as pl
from jax.experimental.pallas import tpu as pltpu
from jax.sharding import PartitionSpec as P

ROWS = 16
COLS = 16
CHIPS = ROWS // 2
ROUNDS = CHIPS // 2
SLOTS = CHIPS
LANES = 256


def held_from(chip, core, slot):
    steps = (slot + 1) // 2
    parity = core if slot % 2 or slot == 0 else 1 - core
    away = -steps if core == 0 else steps
    return 2 * ((chip + away) % CHIPS) + parity


def every_place():
    for chip in range(CHIPS):
        for core in range(2):
            for slot in range(SLOTS):
                for other in range(2):
                    yield chip, core, slot, other


def depth_moves():
    return [
        (
            (2 * chip + (core ^ other)) * COLS + held_from(chip, core, slot),
            (2 * chip + core) * COLS + 2 * slot + other,
        )
        for chip, core, slot, other in every_place()
    ]


def token_moves():
    return [
        (
            held_from(chip, core, slot) * COLS + 2 * chip + (core ^ other),
            (2 * chip + core) * COLS + 2 * slot + other,
        )
        for chip, core, slot, other in every_place()
    ]


def ring_moves(cross):
    moves = []
    for chip in range(CHIPS):
        moves.append((2 * chip + cross, 2 * ((chip + 1) % CHIPS)))
        moves.append((2 * chip + 1 - cross, 2 * ((chip - 1) % CHIPS) + 1))
    return moves


def ring(block):
    slots = [block]
    same = cross = block
    for step in range(1, ROUNDS + 1):
        if step == ROUNDS:
            same = after(same, cross)
        same = lax.ppermute(same, "row", ring_moves(0))
        slots.append(same)
        if step < ROUNDS:
            cross = lax.ppermute(cross, "row", ring_moves(1 if step == 1 else 0))
            slots.append(cross)
    return slots


def to_other_core(value):
    return lax.ppermute(value, "row", [(row, row ^ 1) for row in range(ROWS)])


def to_all_cols(block):
    copies = jnp.broadcast_to(block[None], (COLS,) + block.shape)
    return lax.all_to_all(copies, "col", 0, 0, tiled=True)


def after(value, *others):
    return lax.optimization_barrier((value,) + others)[0]


def input_grad_kernel(own_ref, other_ref, *refs):
    *weight_refs, pieces_ref = refs
    for slot, weight_ref in enumerate(weight_refs):
        for half, grad_ref in enumerate((own_ref, other_ref)):
            pieces_ref[2 * slot + half] = lax.dot_general(
                weight_ref[...],
                grad_ref[...],
                (((1,), (1,)), ((), ())),
                preferred_element_type=jnp.float32,
            ).astype(jnp.bfloat16)


def input_grad_pieces(own, other, weights):
    depth, hidden_units = weights[0].shape
    tokens = own.shape[0]
    moved = (SLOTS * depth * hidden_units + 2 * own.size + SLOTS * depth * 2 * tokens) * 2
    return pl.pallas_call(
        input_grad_kernel,
        out_shape=jax.ShapeDtypeStruct((2 * SLOTS, depth, tokens), jnp.bfloat16),
        in_specs=[pl.BlockSpec(memory_space=pltpu.VMEM)] * (2 + SLOTS),
        out_specs=pl.BlockSpec(memory_space=pltpu.VMEM),
        compiler_params=pltpu.CompilerParams(vmem_limit_bytes=16 * 2**20),
        cost_estimate=pl.CostEstimate(
            flops=4 * SLOTS * depth * hidden_units * tokens,
            bytes_accessed=moved,
            transcendentals=0,
        ),
    )(own, other, *weights)


def token_sum_kernel(slots, first, block_ref, *refs):
    grad_refs = refs[: len(slots)]
    before = None if first else refs[len(slots) : len(slots) + 2]
    outs = refs[-2:]
    hidden_units = grad_refs[0].shape[1]
    for half in range(2):
        for start in range(0, hidden_units, LANES):
            units = pl.ds(start, LANES)
            total = None if first else before[half][:, units]
            for slot, grad_ref in zip(slots, grad_refs):
                term = jnp.dot(
                    block_ref[2 * slot + half],
                    grad_ref[:, units],
                    preferred_element_type=jnp.float32,
                )
                total = term if total is None else total + term
            outs[half][:, units] = total.astype(outs[half].dtype)


def token_sum(slots, blocks, grads, before, kinds):
    depth, tokens = blocks.shape[1:]
    hidden_units = grads[0].shape[1]
    operands = (blocks, *grads, *before)
    return pl.pallas_call(
        functools.partial(token_sum_kernel, slots, not before),
        out_shape=[jax.ShapeDtypeStruct((depth, hidden_units), kind) for kind in kinds],
        in_specs=[pl.BlockSpec(memory_space=pltpu.VMEM)] * len(operands),
        out_specs=[pl.BlockSpec(memory_space=pltpu.VMEM)] * 2,
        compiler_params=pltpu.CompilerParams(vmem_limit_bytes=16 * 2**20),
        cost_estimate=pl.CostEstimate(
            flops=4 * len(slots) * depth * hidden_units * tokens,
            bytes_accessed=2 * (blocks.size + len(slots) * tokens * hidden_units)
            + 4 * 2 * depth * hidden_units,
            transcendentals=0,
        ),
    )(*operands)


def per_device(features, up_weight, out_grad):
    tokens, depth = features.shape
    hidden_units = up_weight.shape[1]
    features = features.T
    weights = ring(up_weight)
    by_depth = lax.ppermute(features, ("row", "col"), depth_moves())
    by_token = lax.ppermute(features, ("row", "col"), token_moves())
    both_ways = jnp.concatenate([by_depth, by_token], axis=0)
    both_ways = to_all_cols(after(both_ways, weights[1]))
    by_depth, by_token = both_ways[:, :depth], both_ways[:, depth:]

    both = 0.0
    for slot, weight in enumerate(weights):
        block = jnp.concatenate([by_depth[2 * slot], by_depth[2 * slot + 1]], axis=1)
        both += lax.dot_general(
            block, weight, (((0,), (0,)), ((), ())), preferred_element_type=jnp.float32
        )
    hidden = both[:tokens] + to_other_core(both[tokens:].astype(jnp.bfloat16)).astype(jnp.float32)
    normal_cdf = 0.5 * (1.0 + jax.scipy.special.erf(hidden / math.sqrt(2.0)))
    density = jnp.exp(-0.5 * hidden * hidden) / math.sqrt(2.0 * math.pi)
    gelu_out = (hidden * normal_cdf).astype(jnp.bfloat16)
    hidden_grad = (out_grad.astype(jnp.float32) * (normal_cdf + hidden * density)).astype(
        jnp.bfloat16
    )

    grads = ring(hidden_grad)
    own_grad = after(hidden_grad, grads[1], grads[2])
    pieces = input_grad_pieces(own_grad, to_other_core(hidden_grad), weights)
    pieces = lax.all_to_all(pieces, "col", 0, 0, tiled=True)
    feature_grad = jnp.sum(pieces.astype(jnp.float32), axis=0).astype(jnp.bfloat16)
    feature_grad = lax.ppermute(
        feature_grad, ("row", "col"), [(to, source) for source, to in depth_moves()]
    )

    split = SLOTS - 3
    wide = jnp.float32
    sums = token_sum(range(split), by_token, grads[:split], (), (wide, wide))
    last = after(grads[-1], feature_grad)
    own, other = token_sum(
        range(split, SLOTS), by_token, [*grads[split:-1], last], sums, (wide, jnp.bfloat16)
    )
    own = (own + to_other_core(other).astype(jnp.float32)).astype(jnp.bfloat16)
    replica = lax.ppermute(own, "dp", [(0, 1), (1, 0)])
    weight_grad = own.astype(jnp.float32) + replica.astype(jnp.float32)
    feature_grad = feature_grad.T
    return (gelu_out, feature_grad, weight_grad)


def solution(mesh):
    placed = (P(("dp", "row"), "col"), P("row", "col"), P(("dp", "row"), "col"))
    return jax.shard_map(
        per_device,
        mesh=mesh,
        in_specs=placed,
        out_specs=(P(("dp", "row"), "col"), P(("dp", "row"), "col"), P("row", "col")),
        check_vma=False,
    )
```

```python
import functools
import math

import jax
import jax.numpy as jnp
from jax import lax
from jax.experimental import pallas as pl
from jax.experimental.pallas import tpu as pltpu
from jax.sharding import PartitionSpec as P

ROWS = 16
COLS = 16
CHIPS = ROWS // 2
ROUNDS = CHIPS // 2
SLOTS = CHIPS
LANES = 256
EXCHANGE_FLOPS = 10**10


def held_from(chip, core, slot):
    steps = (slot + 1) // 2
    parity = core if slot % 2 or slot == 0 else 1 - core
    away = -steps if core == 0 else steps
    return 2 * ((chip + away) % CHIPS) + parity


def every_place():
    for chip in range(CHIPS):
        for core in range(2):
            for slot in range(SLOTS):
                for other in range(2):
                    yield chip, core, slot, other


def depth_moves():
    return [
        (
            (2 * chip + (core ^ other)) * COLS + held_from(chip, core, slot),
            (2 * chip + core) * COLS + 2 * slot + other,
        )
        for chip, core, slot, other in every_place()
    ]


def token_moves():
    return [
        (
            held_from(chip, core, slot) * COLS + 2 * chip + (core ^ other),
            (2 * chip + core) * COLS + 2 * slot + other,
        )
        for chip, core, slot, other in every_place()
    ]


def ring_moves(cross):
    moves = []
    for chip in range(CHIPS):
        moves.append((2 * chip + cross, 2 * ((chip + 1) % CHIPS)))
        moves.append((2 * chip + 1 - cross, 2 * ((chip - 1) % CHIPS) + 1))
    return moves


def ring(block):
    slots = [block]
    same = cross = block
    for step in range(1, ROUNDS + 1):
        if step == ROUNDS:
            same = after(same, cross)
        same = lax.ppermute(same, "row", ring_moves(0))
        slots.append(same)
        if step < ROUNDS:
            cross = lax.ppermute(cross, "row", ring_moves(1 if step == 1 else 0))
            slots.append(cross)
    return slots


def to_other_core(value):
    return lax.ppermute(value, "row", [(row, row ^ 1) for row in range(ROWS)])


def after(value, *others):
    return lax.optimization_barrier((value,) + others)[0]


def copies_kernel(first_ref, second_ref, copies_ref):
    depth = first_ref.shape[0]
    for col in range(COLS):
        copies_ref[col, :depth] = first_ref[...]
        copies_ref[col, depth:] = second_ref[...]


def copies_for_cols(first, second):
    depth, tokens = first.shape
    return pl.pallas_call(
        copies_kernel,
        out_shape=jax.ShapeDtypeStruct((COLS, 2 * depth, tokens), first.dtype),
        in_specs=[pl.BlockSpec(memory_space=pltpu.VMEM)] * 2,
        out_specs=pl.BlockSpec(memory_space=pltpu.VMEM),
        compiler_params=pltpu.CompilerParams(vmem_limit_bytes=16 * 2**20),
        cost_estimate=pl.CostEstimate(
            flops=EXCHANGE_FLOPS,
            bytes_accessed=4 * COLS * depth * tokens,
            transcendentals=0,
        ),
    )(first, second)


def input_grad_kernel(own_ref, other_ref, *refs):
    *weight_refs, pieces_ref = refs
    for slot, weight_ref in enumerate(weight_refs):
        for half, grad_ref in enumerate((own_ref, other_ref)):
            pieces_ref[2 * slot + half] = lax.dot_general(
                weight_ref[...],
                grad_ref[...],
                (((1,), (1,)), ((), ())),
                preferred_element_type=jnp.float32,
            ).astype(jnp.bfloat16)


def input_grad_pieces(own, other, weights):
    depth, hidden_units = weights[0].shape
    tokens = own.shape[0]
    moved = (SLOTS * depth * hidden_units + 2 * own.size + SLOTS * depth * 2 * tokens) * 2
    return pl.pallas_call(
        input_grad_kernel,
        out_shape=jax.ShapeDtypeStruct((2 * SLOTS, depth, tokens), jnp.bfloat16),
        in_specs=[pl.BlockSpec(memory_space=pltpu.VMEM)] * (2 + SLOTS),
        out_specs=pl.BlockSpec(memory_space=pltpu.VMEM),
        compiler_params=pltpu.CompilerParams(vmem_limit_bytes=16 * 2**20),
        cost_estimate=pl.CostEstimate(
            flops=4 * SLOTS * depth * hidden_units * tokens + EXCHANGE_FLOPS,
            bytes_accessed=moved,
            transcendentals=0,
        ),
    )(own, other, *weights)


def token_sum_kernel(slots, first, block_ref, *refs):
    grad_refs = refs[: len(slots)]
    before = None if first else refs[len(slots) : len(slots) + 2]
    outs = refs[-2:]
    hidden_units = grad_refs[0].shape[1]
    for half in range(2):
        for start in range(0, hidden_units, LANES):
            units = pl.ds(start, LANES)
            total = None if first else before[half][:, units]
            for slot, grad_ref in zip(slots, grad_refs):
                term = jnp.dot(
                    block_ref[2 * slot + half],
                    grad_ref[:, units],
                    preferred_element_type=jnp.float32,
                )
                total = term if total is None else total + term
            outs[half][:, units] = total.astype(outs[half].dtype)


def token_sum(slots, blocks, grads, before, kinds):
    depth, tokens = blocks.shape[1:]
    hidden_units = grads[0].shape[1]
    operands = (blocks, *grads, *before)
    return pl.pallas_call(
        functools.partial(token_sum_kernel, slots, not before),
        out_shape=[jax.ShapeDtypeStruct((depth, hidden_units), kind) for kind in kinds],
        in_specs=[pl.BlockSpec(memory_space=pltpu.VMEM)] * len(operands),
        out_specs=[pl.BlockSpec(memory_space=pltpu.VMEM)] * 2,
        compiler_params=pltpu.CompilerParams(vmem_limit_bytes=16 * 2**20),
        cost_estimate=pl.CostEstimate(
            flops=4 * len(slots) * depth * hidden_units * tokens,
            bytes_accessed=2 * (blocks.size + len(slots) * tokens * hidden_units)
            + 4 * 2 * depth * hidden_units,
            transcendentals=0,
        ),
    )(*operands)


def per_device(features, up_weight, out_grad):
    tokens, depth = features.shape
    hidden_units = up_weight.shape[1]
    features = features.T
    weights = ring(up_weight)
    by_depth = lax.ppermute(features, ("row", "col"), depth_moves())
    by_token = lax.ppermute(features, ("row", "col"), token_moves())
    both_ways = lax.all_to_all(copies_for_cols(by_depth, by_token), "col", 0, 0, tiled=True)
    by_depth, by_token = both_ways[:, :depth], both_ways[:, depth:]

    both = 0.0
    for slot, weight in enumerate(weights):
        block = jnp.concatenate([by_depth[2 * slot], by_depth[2 * slot + 1]], axis=1)
        both += lax.dot_general(
            block, weight, (((0,), (0,)), ((), ())), preferred_element_type=jnp.float32
        )
    hidden = both[:tokens] + to_other_core(both[tokens:].astype(jnp.bfloat16)).astype(jnp.float32)
    normal_cdf = 0.5 * (1.0 + jax.scipy.special.erf(hidden / math.sqrt(2.0)))
    density = jnp.exp(-0.5 * hidden * hidden) / math.sqrt(2.0 * math.pi)
    gelu_out = (hidden * normal_cdf).astype(jnp.bfloat16)
    hidden_grad = (out_grad.astype(jnp.float32) * (normal_cdf + hidden * density)).astype(
        jnp.bfloat16
    )

    grads = ring(hidden_grad)
    own_grad = after(hidden_grad, grads[1], grads[2])
    pieces = input_grad_pieces(own_grad, to_other_core(hidden_grad), weights)
    pieces = lax.all_to_all(pieces, "col", 0, 0, tiled=True)
    feature_grad = jnp.sum(pieces.astype(jnp.float32), axis=0).astype(jnp.bfloat16)
    feature_grad = lax.ppermute(
        feature_grad, ("row", "col"), [(to, source) for source, to in depth_moves()]
    )

    split = SLOTS - 3
    wide = jnp.float32
    sums = token_sum(range(split), by_token, grads[:split], (), (wide, wide))
    last = after(grads[-1], feature_grad)
    own, other = token_sum(
        range(split, SLOTS), by_token, [*grads[split:-1], last], sums, (wide, jnp.bfloat16)
    )
    own = (own + to_other_core(other).astype(jnp.float32)).astype(jnp.bfloat16)
    replica = lax.ppermute(own, "dp", [(0, 1), (1, 0)])
    weight_grad = own.astype(jnp.float32) + replica.astype(jnp.float32)
    feature_grad = feature_grad.T
    return (gelu_out, feature_grad, weight_grad)


def solution(mesh):
    placed = (P(("dp", "row"), "col"), P("row", "col"), P(("dp", "row"), "col"))
    return jax.shard_map(
        per_device,
        mesh=mesh,
        in_specs=placed,
        out_specs=(P(("dp", "row"), "col"), P(("dp", "row"), "col"), P("row", "col")),
        check_vma=False,
    )
```

```python
import functools
import math

import jax
import jax.numpy as jnp
from jax import lax
from jax.experimental import pallas as pl
from jax.experimental.pallas import tpu as pltpu
from jax.sharding import PartitionSpec as P

ROWS = 16
COLS = 16
LANES = 256
VMEM_BYTES = 32 * 2**20


def after(value, *others):
    return lax.optimization_barrier((value,) + others)[0]


def local_kernel(kernel, out_shape, flops, operands):
    moved = sum(x.size * x.dtype.itemsize for x in (*operands, out_shape))
    return pl.pallas_call(
        kernel,
        out_shape=out_shape,
        in_specs=[pl.BlockSpec(memory_space=pltpu.VMEM)] * len(operands),
        out_specs=pl.BlockSpec(memory_space=pltpu.VMEM),
        compiler_params=pltpu.CompilerParams(vmem_limit_bytes=VMEM_BYTES),
        cost_estimate=pl.CostEstimate(flops=flops, bytes_accessed=moved, transcendentals=0),
    )(*operands)


def input_grad_kernel(weight_ref, grad_ref, pieces_ref):
    depth = pieces_ref.shape[1]
    for col in range(COLS):
        pieces_ref[col] = lax.dot_general(
            weight_ref[pl.ds(col * depth, depth), :],
            grad_ref[...],
            (((1,), (1,)), ((), ())),
            preferred_element_type=jnp.float32,
        ).astype(jnp.bfloat16)


def input_grad_pieces(weight, grad):
    tokens, hidden_units = grad.shape
    depth = weight.shape[0] // COLS
    out_shape = jax.ShapeDtypeStruct((COLS, depth, tokens), jnp.bfloat16)
    flops = 2 * weight.size * tokens
    return local_kernel(input_grad_kernel, out_shape, flops, (weight, grad))


def token_sum_kernel(block_ref, grad_ref, total_ref):
    rows, _, tokens = block_ref.shape
    for start in range(0, total_ref.shape[1], LANES):
        units = pl.ds(start, LANES)
        total = None
        for row in range(rows):
            term = jnp.dot(
                block_ref[row],
                grad_ref[pl.ds(row * tokens, tokens), units],
                preferred_element_type=jnp.float32,
            )
            total = term if total is None else total + term
        total_ref[:, units] = total.astype(total_ref.dtype)


def token_sum(blocks, grads):
    depth = blocks.shape[1]
    out_shape = jax.ShapeDtypeStruct((depth, grads.shape[1]), jnp.bfloat16)
    flops = 2 * depth * grads.size
    return local_kernel(token_sum_kernel, out_shape, flops, (blocks, grads))


def per_device(features, up_weight, out_grad):
    tokens, depth = features.shape
    features = features.T
    weight = lax.all_gather(up_weight, "row", axis=0, tiled=True)
    swap = [(r * COLS + c, c * COLS + r) for r in range(ROWS) for c in range(COLS)]
    turned = lax.ppermute(features, ("row", "col"), swap)
    block = jnp.concatenate([features, turned], axis=0)
    copies = jnp.broadcast_to(block[None], (COLS,) + block.shape)
    both_ways = lax.all_to_all(copies, "col", 0, 0, tiled=True)
    by_depth = both_ways[:, :depth].reshape(COLS * depth, tokens)
    by_token = both_ways[:, depth:]

    hidden = lax.dot_general(
        by_depth, weight, (((0,), (0,)), ((), ())), preferred_element_type=jnp.float32
    )
    normal_cdf = 0.5 * (1.0 + jax.scipy.special.erf(hidden / math.sqrt(2.0)))
    density = jnp.exp(-0.5 * hidden * hidden) / math.sqrt(2.0 * math.pi)
    gelu_out = (hidden * normal_cdf).astype(jnp.bfloat16)
    hidden_grad = (out_grad.astype(jnp.float32) * (normal_cdf + hidden * density)).astype(
        jnp.bfloat16
    )
    grads = lax.all_gather(hidden_grad, "row", axis=0, tiled=True)

    pieces = input_grad_pieces(weight, hidden_grad)
    pieces = lax.all_to_all(pieces, "col", 0, 0, tiled=True)
    feature_grad = jnp.sum(pieces.astype(jnp.float32), axis=0).astype(jnp.bfloat16)

    own = token_sum(by_token, after(grads, feature_grad))
    replica = lax.ppermute(own, "dp", [(0, 1), (1, 0)])
    weight_grad = own.astype(jnp.float32) + replica.astype(jnp.float32)
    return (gelu_out, feature_grad.T, weight_grad)


def solution(mesh):
    placed = (P(("dp", "row"), "col"), P("row", "col"), P(("dp", "row"), "col"))
    return jax.shard_map(
        per_device,
        mesh=mesh,
        in_specs=placed,
        out_specs=(P(("dp", "row"), "col"), P(("dp", "row"), "col"), P("row", "col")),
        check_vma=False,
    )
```

```python
import math

import jax
import jax.numpy as jnp
from jax import lax
from jax.experimental import pallas as pl
from jax.experimental.pallas import tpu as pltpu
from jax.sharding import PartitionSpec as P

ROWS = 16
COLS = 16
CHIPS = ROWS // 2
ROUNDS = CHIPS // 2
EARLY = 5
LANES = 256
RING_UNITS = 768
VMEM_BYTES = 32 * 2**20


def after(value, *others):
    return lax.optimization_barrier((value,) + others)[0]


def held_from(chip, core, slot):
    steps = (slot + 1) // 2
    parity = core if slot % 2 or slot == 0 else 1 - core
    away = -steps if core == 0 else steps
    return 2 * ((chip + away) % CHIPS) + parity


def places():
    table = []
    for row in range(ROWS):
        chip, core = divmod(row, 2)
        mine = [held_from(chip, core, slot) for slot in range(CHIPS)]
        other = [held_from(chip, 1 - core, slot) for slot in range(CHIPS)]
        table.append(mine + other)
    return jnp.array(table, jnp.int32)[lax.axis_index("row")]


def ring_moves(cross):
    moves = []
    for chip in range(CHIPS):
        moves.append((2 * chip + cross, 2 * ((chip + 1) % CHIPS)))
        moves.append((2 * chip + 1 - cross, 2 * ((chip - 1) % CHIPS) + 1))
    return moves


def to_other_core(value):
    return lax.ppermute(value, "row", [(row, row ^ 1) for row in range(ROWS)])


def ring_gather(block):
    mine = [block]
    same = cross = block
    for step in range(1, ROUNDS + 1):
        if step == ROUNDS:
            same = after(same, cross)
        same = lax.ppermute(same, "row", ring_moves(0))
        mine.append(same)
        if step < ROUNDS:
            cross = lax.ppermute(cross, "row", ring_moves(1 if step == 1 else 0))
            mine.append(cross)
    early = to_other_core(jnp.concatenate(mine[:EARLY]))
    late = to_other_core(jnp.concatenate(mine[EARLY:]))
    return mine + [early, late]


def ring_blocks(refs, depth):
    *mine, early, late = refs
    for ref in mine:
        yield ref[...]
    for stack in (early, late):
        for start in range(0, stack.shape[0], depth):
            yield stack[pl.ds(start, depth), :]


def local_kernel(kernel, out_shape, flops, operands, indices=None):
    moved = sum(x.size * x.dtype.itemsize for x in (*operands, out_shape))
    in_specs = [pl.BlockSpec(memory_space=pltpu.VMEM)] * len(operands)
    if indices is not None:
        in_specs = [pl.BlockSpec(memory_space=pltpu.SMEM)] + in_specs
        operands = (indices, *operands)
    return pl.pallas_call(
        kernel,
        out_shape=out_shape,
        in_specs=in_specs,
        out_specs=pl.BlockSpec(memory_space=pltpu.VMEM),
        compiler_params=pltpu.CompilerParams(vmem_limit_bytes=VMEM_BYTES),
        cost_estimate=pl.CostEstimate(flops=flops, bytes_accessed=moved, transcendentals=0),
    )(*operands)


def ring_hidden_kernel(place_ref, by_depth_ref, *refs):
    *weight_refs, hidden_ref = refs
    depth = by_depth_ref.shape[1]
    total = None
    for slot, weight in enumerate(ring_blocks(weight_refs, depth)):
        term = lax.dot_general(
            by_depth_ref[place_ref[slot]],
            weight,
            (((0,), (0,)), ((), ())),
            preferred_element_type=jnp.float32,
        )
        total = term if total is None else total + term
    hidden_ref[...] = total


def input_grad_kernel(place_ref, ring_grad_ref, grad_ref, weight_ref, *refs):
    *ring_refs, pieces_ref = refs
    depth = pieces_ref.shape[1]
    contract_last = (((1,), (1,)), ((), ()))
    for slot, ring_weight in enumerate(ring_blocks(ring_refs, depth)):
        place = place_ref[slot]
        start = pl.multiple_of(place * depth, depth)
        first = lax.dot_general(
            ring_weight, ring_grad_ref[...], contract_last, preferred_element_type=jnp.float32
        )
        second = lax.dot_general(
            weight_ref[pl.ds(start, depth), :],
            grad_ref[...],
            contract_last,
            preferred_element_type=jnp.float32,
        )
        pieces_ref[place] = (first + second).astype(jnp.bfloat16)


def ring_sum_kernel(place_ref, by_token_ref, *refs):
    *grad_refs, total_ref = refs
    tokens = by_token_ref.shape[2]
    total = None
    for slot, grad in enumerate(ring_blocks(grad_refs, tokens)):
        term = jnp.dot(by_token_ref[place_ref[slot]], grad, preferred_element_type=jnp.float32)
        total = term if total is None else total + term
    total_ref[...] = total.astype(total_ref.dtype)


def token_sum_kernel(by_token_ref, grad_ref, total_ref):
    rows, _, tokens = by_token_ref.shape
    for start in range(0, total_ref.shape[1], LANES):
        units = pl.ds(start, LANES)
        total = None
        for row in range(rows):
            term = jnp.dot(
                by_token_ref[row],
                grad_ref[pl.ds(row * tokens, tokens), units],
                preferred_element_type=jnp.float32,
            )
            total = term if total is None else total + term
        total_ref[:, units] = total.astype(total_ref.dtype)


def gelu_parts(hidden, out_grad):
    normal_cdf = 0.5 * (1.0 + jax.scipy.special.erf(hidden / math.sqrt(2.0)))
    density = jnp.exp(-0.5 * hidden * hidden) / math.sqrt(2.0 * math.pi)
    gelu_out = (hidden * normal_cdf).astype(jnp.bfloat16)
    hidden_grad = out_grad.astype(jnp.float32) * (normal_cdf + hidden * density)
    return gelu_out, hidden_grad.astype(jnp.bfloat16)


def replica_sum(own):
    replica = lax.ppermute(own, "dp", [(0, 1), (1, 0)])
    return own.astype(jnp.float32) + replica.astype(jnp.float32)


def per_device(features, up_weight, out_grad):
    tokens, depth = features.shape
    rest = up_weight.shape[1] - RING_UNITS
    place = places()
    features = features.T
    weight = lax.all_gather(up_weight[:, RING_UNITS:], "row", axis=0, tiled=True)
    ring_weight = ring_gather(up_weight[:, :RING_UNITS])
    swap = [(r * COLS + c, c * COLS + r) for r in range(ROWS) for c in range(COLS)]
    turned = lax.ppermute(features, ("row", "col"), swap)
    block = jnp.concatenate([features, turned], axis=0)
    copies = jnp.broadcast_to(block[None], (COLS,) + block.shape)
    both_ways = lax.all_to_all(copies, "col", 0, 0, tiled=True)
    by_depth, by_token = both_ways[:, :depth], both_ways[:, depth:]

    ring_hidden = local_kernel(
        ring_hidden_kernel,
        jax.ShapeDtypeStruct((tokens, RING_UNITS), jnp.float32),
        2 * tokens * ROWS * depth * RING_UNITS,
        (by_depth, *ring_weight),
        place,
    )
    ring_gelu, ring_grad = gelu_parts(ring_hidden, out_grad[:, :RING_UNITS])
    ring_grads = ring_gather(ring_grad)

    hidden = lax.dot_general(
        by_depth.reshape(COLS * depth, tokens),
        weight,
        (((0,), (0,)), ((), ())),
        preferred_element_type=jnp.float32,
    )
    gelu_out, grad = gelu_parts(hidden, out_grad[:, RING_UNITS:])
    grads = lax.all_gather(grad, "row", axis=0, tiled=True)

    pieces = local_kernel(
        input_grad_kernel,
        jax.ShapeDtypeStruct((COLS, depth, tokens), jnp.bfloat16),
        2 * tokens * ROWS * depth * (RING_UNITS + rest),
        (ring_grad, grad, weight, *ring_weight),
        place,
    )
    pieces = lax.all_to_all(pieces, "col", 0, 0, tiled=True)
    feature_grad = jnp.sum(pieces.astype(jnp.float32), axis=0).astype(jnp.bfloat16)

    ring_own = local_kernel(
        ring_sum_kernel,
        jax.ShapeDtypeStruct((depth, RING_UNITS), jnp.bfloat16),
        2 * tokens * ROWS * depth * RING_UNITS,
        (by_token, *ring_grads),
        place,
    )
    ring_total = replica_sum(ring_own)
    own = local_kernel(
        token_sum_kernel,
        jax.ShapeDtypeStruct((depth, rest), jnp.bfloat16),
        2 * tokens * ROWS * depth * rest,
        (by_token, after(grads, feature_grad)),
    )
    total = replica_sum(own)
    gelu_out = jnp.concatenate([ring_gelu, gelu_out], axis=1)
    weight_grad = jnp.concatenate([ring_total, total], axis=1)
    return (gelu_out, feature_grad.T, weight_grad)


def solution(mesh):
    placed = (P(("dp", "row"), "col"), P("row", "col"), P(("dp", "row"), "col"))
    return jax.shard_map(
        per_device,
        mesh=mesh,
        in_specs=placed,
        out_specs=(P(("dp", "row"), "col"), P(("dp", "row"), "col"), P("row", "col")),
        check_vma=False,
    )
```

```python
import functools
import math

import jax
import jax.numpy as jnp
from jax import lax
from jax.experimental import pallas as pl
from jax.experimental.pallas import tpu as pltpu
from jax.sharding import PartitionSpec as P

ROWS = 16
COLS = 16
SIDE = 4
CHIPS = ROWS // 2
ROUNDS = CHIPS // 2
SLOTS = CHIPS
SPLIT = 5
LANES = 256
VMEM_BYTES = 24 * 2**20


def after(value, *others):
    return lax.optimization_barrier((value,) + others)[0]


def held_from(chip, core, slot):
    steps = (slot + 1) // 2
    parity = core if slot % 2 or slot == 0 else 1 - core
    away = -steps if core == 0 else steps
    return 2 * ((chip + away) % CHIPS) + parity


def every_place():
    for chip in range(CHIPS):
        for core in range(2):
            for slot in range(SLOTS):
                for other in range(2):
                    yield chip, core, slot, other


def depth_moves():
    return [
        (
            (2 * chip + (core ^ other)) * COLS + held_from(chip, core, slot),
            (2 * chip + core) * COLS + 2 * slot + other,
        )
        for chip, core, slot, other in every_place()
    ]


def token_moves():
    return [
        (
            held_from(chip, core, slot) * COLS + 2 * chip + (core ^ other),
            (2 * chip + core) * COLS + 2 * slot + other,
        )
        for chip, core, slot, other in every_place()
    ]


def ring_moves(cross):
    moves = []
    for chip in range(CHIPS):
        moves.append((2 * chip + cross, 2 * ((chip + 1) % CHIPS)))
        moves.append((2 * chip + 1 - cross, 2 * ((chip - 1) % CHIPS) + 1))
    return moves


def ring(block):
    slots = [block]
    same = cross = block
    for step in range(1, ROUNDS + 1):
        if step == ROUNDS:
            same = after(same, cross)
        same = lax.ppermute(same, "row", ring_moves(0))
        slots.append(same)
        if step < ROUNDS:
            cross = lax.ppermute(cross, "row", ring_moves(1 if step == 1 else 0))
            slots.append(cross)
    return slots


def to_other_core(value):
    return lax.ppermute(value, "row", [(row, row ^ 1) for row in range(ROWS)])


def along_y(value, steps):
    moves = [(c, (c + SIDE * steps) % COLS) for c in range(COLS)]
    return lax.ppermute(value, "col", moves)


def along_x(value, steps):
    moves = [(c, c // SIDE * SIDE + (c + steps) % SIDE) for c in range(COLS)]
    return lax.ppermute(value, "col", moves)


def from_all_cols(block):
    line = jnp.stack([block] + [along_y(block, d) for d in range(1, SIDE)])
    return jnp.concatenate([line] + [along_x(line, e) for e in range(1, SIDE)])


def sum_to_cols(pieces):
    line = pieces[:SIDE].astype(jnp.float32)
    for e in range(1, SIDE):
        line += along_x(pieces[SIDE * e : SIDE * (e + 1)], e).astype(jnp.float32)
    line = line.astype(jnp.bfloat16)
    total = line[0].astype(jnp.float32)
    for d in range(1, SIDE):
        total += along_y(line[d], d).astype(jnp.float32)
    return total.astype(jnp.bfloat16)


def places(sign):
    tables = []
    for col in range(COLS):
        y, x = divmod(col, SIDE)
        tables.append(
            [
                SIDE * ((sign * (c % SIDE - x)) % SIDE) + (sign * (c // SIDE - y)) % SIDE
                for c in range(COLS)
            ]
        )
    return jnp.array(tables, jnp.int32)[lax.axis_index("col")]


def local_kernel(kernel, out_shapes, flops, place, operands):
    moved = sum(x.size * x.dtype.itemsize for x in (*operands, *out_shapes))
    vmem = pl.BlockSpec(memory_space=pltpu.VMEM)
    return pl.pallas_call(
        kernel,
        out_shape=out_shapes,
        in_specs=[pl.BlockSpec(memory_space=pltpu.SMEM)] + [vmem] * len(operands),
        out_specs=[vmem] * len(out_shapes),
        compiler_params=pltpu.CompilerParams(vmem_limit_bytes=VMEM_BYTES),
        cost_estimate=pl.CostEstimate(flops=flops, bytes_accessed=moved, transcendentals=0),
    )(place, *operands)


def slot_sum_kernel(slots, by_depth, place_ref, block_ref, *refs):
    value_refs = refs[: len(slots)]
    before = refs[len(slots) : -2]
    outs = refs[-2:]
    depth = block_ref.shape[1] // 2
    for half in range(2):
        blocks = []
        for slot in slots:
            rows = pl.ds(0 if by_depth else depth, depth)
            blocks.append(block_ref[place_ref[2 * slot + half], rows, :])
        for start in range(0, value_refs[0].shape[1], LANES):
            units = pl.ds(start, LANES)
            total = before[half][:, units] if before else None
            for block, value_ref in zip(blocks, value_refs):
                term = lax.dot_general(
                    block,
                    value_ref[:, units],
                    (((0 if by_depth else 1,), (0,)), ((), ())),
                    preferred_element_type=jnp.float32,
                )
                total = term if total is None else total + term
            outs[half][:, units] = total.astype(outs[half].dtype)


def slot_sums(by_depth, place, blocks, values, last):
    depth, tokens = blocks.shape[1] // 2, blocks.shape[2]
    rows = tokens if by_depth else depth
    width = values[0].shape[1]
    wide = jax.ShapeDtypeStruct((rows, width), jnp.float32)
    narrow = jax.ShapeDtypeStruct((rows, width), jnp.bfloat16)
    sums = ()
    parts = (range(SPLIT), (wide, wide)), (range(SPLIT, SLOTS), (wide, narrow))
    for slots, out_shapes in parts:
        given = [values[slot] for slot in slots]
        if sums:
            given[-1] = last(given[-1])
        sums = local_kernel(
            functools.partial(slot_sum_kernel, slots, by_depth),
            out_shapes,
            4 * len(slots) * depth * tokens * width,
            place,
            (blocks, *given, *sums),
        )
    return sums


def input_grad_kernel(place_ref, own_ref, other_ref, *refs):
    *weight_refs, pieces_ref = refs
    for slot, weight_ref in enumerate(weight_refs):
        for half, grad_ref in enumerate((own_ref, other_ref)):
            pieces_ref[place_ref[2 * slot + half]] = lax.dot_general(
                weight_ref[...],
                grad_ref[...],
                (((1,), (1,)), ((), ())),
                preferred_element_type=jnp.float32,
            ).astype(jnp.bfloat16)


def per_device(features, up_weight, out_grad):
    tokens, depth = features.shape
    hidden_units = up_weight.shape[1]
    back, ahead = places(-1), places(1)
    features = features.T
    weights = ring(up_weight)
    turned = [
        lax.ppermute(features, ("row", "col"), moves()) for moves in (depth_moves, token_moves)
    ]
    blocks = from_all_cols(jnp.concatenate(turned))

    own, other = slot_sums(True, back, blocks, weights, lambda value: value)
    hidden = own + to_other_core(other).astype(jnp.float32)
    normal_cdf = 0.5 * (1.0 + jax.scipy.special.erf(hidden / math.sqrt(2.0)))
    density = jnp.exp(-0.5 * hidden * hidden) / math.sqrt(2.0 * math.pi)
    gelu_out = (hidden * normal_cdf).astype(jnp.bfloat16)
    hidden_grad = (out_grad.astype(jnp.float32) * (normal_cdf + hidden * density)).astype(
        jnp.bfloat16
    )

    grads = ring(hidden_grad)
    (pieces,) = local_kernel(
        input_grad_kernel,
        [jax.ShapeDtypeStruct((COLS, depth, tokens), jnp.bfloat16)],
        4 * SLOTS * depth * hidden_units * tokens,
        ahead,
        (hidden_grad, to_other_core(hidden_grad), *weights),
    )
    feature_grad = lax.ppermute(
        sum_to_cols(pieces), ("row", "col"), [(to, source) for source, to in depth_moves()]
    )

    own, other = slot_sums(False, back, blocks, grads, lambda value: value)
    own = (own + to_other_core(other).astype(jnp.float32)).astype(jnp.bfloat16)
    own = after(own, feature_grad)
    replica = lax.ppermute(own, "dp", [(0, 1), (1, 0)])
    weight_grad = own.astype(jnp.float32) + replica.astype(jnp.float32)
    return (gelu_out, feature_grad.T, weight_grad)


def solution(mesh):
    placed = (P(("dp", "row"), "col"), P("row", "col"), P(("dp", "row"), "col"))
    return jax.shard_map(
        per_device,
        mesh=mesh,
        in_specs=placed,
        out_specs=(P(("dp", "row"), "col"), P(("dp", "row"), "col"), P("row", "col")),
        check_vma=False,
    )
```

```python
import math

import jax
import jax.numpy as jnp
from jax import lax
from jax.experimental import pallas as pl
from jax.experimental.pallas import tpu as pltpu
from jax.sharding import Mesh
from jax.sharding import PartitionSpec as P

ROWS = 16
COLS = 16
SIDE = 4
LANES = 256
VMEM_BYTES = 32 * 2**20
COL = ("y", "x")


def after(value, *others):
    return lax.optimization_barrier((value,) + others)[0]


def local_kernel(kernel, out_shape, flops, operands):
    moved = sum(x.size * x.dtype.itemsize for x in (*operands, out_shape))
    return pl.pallas_call(
        kernel,
        out_shape=out_shape,
        in_specs=[pl.BlockSpec(memory_space=pltpu.VMEM)] * len(operands),
        out_specs=pl.BlockSpec(memory_space=pltpu.VMEM),
        compiler_params=pltpu.CompilerParams(vmem_limit_bytes=VMEM_BYTES),
        cost_estimate=pl.CostEstimate(flops=flops, bytes_accessed=moved, transcendentals=0),
    )(*operands)


def input_grad_kernel(weight_ref, grad_ref, pieces_ref):
    depth = pieces_ref.shape[2]
    for col in range(COLS):
        pieces_ref[col % SIDE, col // SIDE] = lax.dot_general(
            weight_ref[pl.ds(col * depth, depth), :],
            grad_ref[...],
            (((1,), (1,)), ((), ())),
            preferred_element_type=jnp.float32,
        ).astype(jnp.bfloat16)


def input_grad_pieces(weight, grad):
    depth = weight.shape[0] // COLS
    out_shape = jax.ShapeDtypeStruct((SIDE, SIDE, depth, grad.shape[0]), jnp.bfloat16)
    return local_kernel(input_grad_kernel, out_shape, 2 * weight.size * grad.shape[0], (weight, grad))


def token_sum_kernel(block_ref, grad_ref, total_ref):
    rows, _, tokens = block_ref.shape
    for start in range(0, total_ref.shape[1], LANES):
        units = pl.ds(start, LANES)
        total = None
        for row in range(rows):
            term = jnp.dot(
                block_ref[row],
                grad_ref[pl.ds(row * tokens, tokens), units],
                preferred_element_type=jnp.float32,
            )
            total = term if total is None else total + term
        total_ref[:, units] = total.astype(total_ref.dtype)


def token_sum(blocks, grads):
    depth = blocks.shape[1]
    out_shape = jax.ShapeDtypeStruct((depth, grads.shape[1]), jnp.bfloat16)
    return local_kernel(token_sum_kernel, out_shape, 2 * depth * grads.size, (blocks, grads))


def to_replica(value):
    return lax.ppermute(value, "dp", [(0, 1), (1, 0)])


def to_all_cols(block):
    copies = jnp.broadcast_to(block[None], (COLS,) + block.shape)
    return lax.all_to_all(copies, COL, 0, 0, tiled=True)


def sum_along(pieces, axis):
    pieces = lax.all_to_all(pieces, axis, 0, 0, tiled=True)
    return jnp.sum(pieces.astype(jnp.float32), axis=0).astype(jnp.bfloat16)


def turn_moves(replicas):
    moves = []
    for d in range(2 if replicas else 1):
        for r in range(ROWS):
            for c in range(COLS):
                target = c * COLS + r
                if replicas:
                    target += (1 - d) * ROWS * COLS
                moves.append(((d * ROWS + r) * COLS + c, target))
    return moves


def per_device(features, up_weight, out_grad):
    tokens, depth = features.shape
    half = up_weight.shape[1] // 2
    replica = lax.axis_index("dp")
    features = features.T

    def half_of(value, which):
        return lax.dynamic_slice_in_dim(value, which * half, half, axis=1)

    weight = lax.all_gather(half_of(up_weight, replica), "row", axis=0, tiled=True)
    by_depth = to_all_cols(jnp.concatenate([features, to_replica(features)], axis=1))
    turned = [
        lax.ppermute(features, ("row",) + COL, turn_moves(False)),
        lax.ppermute(features, ("dp", "row") + COL, turn_moves(True)),
    ]
    out_grad = jnp.concatenate(
        [half_of(out_grad, replica), to_replica(half_of(out_grad, 1 - replica))], axis=0
    )

    hidden = lax.dot_general(
        by_depth.reshape(COLS * depth, 2 * tokens),
        weight,
        (((0,), (0,)), ((), ())),
        preferred_element_type=jnp.float32,
    )
    normal_cdf = 0.5 * (1.0 + jax.scipy.special.erf(hidden / math.sqrt(2.0)))
    density = jnp.exp(-0.5 * hidden * hidden) / math.sqrt(2.0 * math.pi)
    gelu_half = (hidden * normal_cdf).astype(jnp.bfloat16)
    hidden_grad = (out_grad.astype(jnp.float32) * (normal_cdf + hidden * density)).astype(
        jnp.bfloat16
    )
    grads = lax.all_gather(hidden_grad, "row", axis=0, tiled=True)

    def halves(mine, other):
        parts = jnp.where(replica == 0, mine, other), jnp.where(replica == 0, other, mine)
        return jnp.concatenate(parts, axis=1)

    gelu_out = halves(gelu_half[:tokens], to_replica(gelu_half[tokens:]))
    by_token = to_all_cols(after(jnp.concatenate(turned, axis=1), hidden_grad))

    pieces = input_grad_pieces(weight, hidden_grad)
    feature_grad = sum_along(sum_along(pieces, "x"), "y")
    feature_grad = feature_grad[:, :tokens].astype(jnp.float32) + to_replica(
        feature_grad[:, tokens:]
    ).astype(jnp.float32)
    feature_grad = feature_grad.astype(jnp.bfloat16).T

    own = token_sum(by_token, grads)
    weight_grad = halves(own, to_replica(own)).astype(jnp.float32)
    return (gelu_out, feature_grad, weight_grad)


def solution(mesh):
    names = ("dp", "row") + COL
    fine = Mesh(mesh.devices.reshape(2, ROWS, SIDE, SIDE), names)
    by_tokens = P(("dp", "row"), COL)
    placed = (by_tokens, P("row", COL), by_tokens)
    return jax.shard_map(
        per_device,
        mesh=fine,
        in_specs=placed,
        out_specs=(by_tokens, by_tokens, P("row", COL)),
        check_vma=False,
    )
```

```python
import math

import jax
import jax.numpy as jnp
from jax import lax
from jax.experimental import pallas as pl
from jax.experimental.pallas import tpu as pltpu
from jax.sharding import Mesh
from jax.sharding import PartitionSpec as P

ROWS = 16
COLS = 16
SIDE = 4
LANES = 256
VMEM_BYTES = 32 * 2**20
COL = ("y", "x")


def after(value, *others):
    return lax.optimization_barrier((value,) + others)[0]


def local_kernel(kernel, out_shape, flops, operands):
    moved = sum(x.size * x.dtype.itemsize for x in (*operands, out_shape))
    return pl.pallas_call(
        kernel,
        out_shape=out_shape,
        in_specs=[pl.BlockSpec(memory_space=pltpu.VMEM)] * len(operands),
        out_specs=pl.BlockSpec(memory_space=pltpu.VMEM),
        compiler_params=pltpu.CompilerParams(vmem_limit_bytes=VMEM_BYTES),
        cost_estimate=pl.CostEstimate(flops=flops, bytes_accessed=moved, transcendentals=0),
    )(*operands)


def both_replicas(block_ref, col):
    y, x = divmod(col, SIDE)
    return jnp.concatenate([block_ref[x, y], block_ref[x, SIDE + y]], axis=1)


def hidden_kernel(block_ref, weight_ref, hidden_ref):
    depth = block_ref.shape[2]
    blocks = [both_replicas(block_ref, col) for col in range(COLS)]
    for start in range(0, hidden_ref.shape[1], LANES):
        units = pl.ds(start, LANES)
        total = None
        for col, block in enumerate(blocks):
            term = lax.dot_general(
                block,
                weight_ref[pl.ds(col * depth, depth), units],
                (((0,), (0,)), ((), ())),
                preferred_element_type=jnp.float32,
            )
            total = term if total is None else total + term
        hidden_ref[:, units] = total


def hidden_sum(blocks, weight):
    tokens = 2 * blocks.shape[3]
    out_shape = jax.ShapeDtypeStruct((tokens, weight.shape[1]), jnp.float32)
    return local_kernel(hidden_kernel, out_shape, 2 * tokens * weight.size, (blocks, weight))


def input_grad_kernel(weight_ref, grad_ref, pieces_ref):
    depth, tokens = pieces_ref.shape[2:]
    for col in range(COLS):
        y, x = divmod(col, SIDE)
        piece = lax.dot_general(
            weight_ref[pl.ds(col * depth, depth), :],
            grad_ref[...],
            (((1,), (1,)), ((), ())),
            preferred_element_type=jnp.float32,
        ).astype(jnp.bfloat16)
        pieces_ref[x, y] = piece[:, :tokens]
        pieces_ref[x, SIDE + y] = piece[:, tokens:]


def input_grad_pieces(weight, grad):
    depth = weight.shape[0] // COLS
    out_shape = jax.ShapeDtypeStruct((SIDE, 2 * SIDE, depth, grad.shape[0] // 2), jnp.bfloat16)
    return local_kernel(input_grad_kernel, out_shape, 2 * weight.size * grad.shape[0], (weight, grad))


def token_sum_kernel(block_ref, grad_ref, total_ref):
    tokens = 2 * block_ref.shape[3]
    blocks = [both_replicas(block_ref, row) for row in range(ROWS)]
    for start in range(0, total_ref.shape[1], LANES):
        units = pl.ds(start, LANES)
        total = None
        for row, block in enumerate(blocks):
            term = jnp.dot(
                block,
                grad_ref[pl.ds(row * tokens, tokens), units],
                preferred_element_type=jnp.float32,
            )
            total = term if total is None else total + term
        total_ref[:, units] = total.astype(total_ref.dtype)


def token_sum(blocks, grads):
    depth = blocks.shape[2]
    out_shape = jax.ShapeDtypeStruct((depth, grads.shape[1]), jnp.bfloat16)
    return local_kernel(token_sum_kernel, out_shape, 2 * depth * grads.size, (blocks, grads))


def to_replica(value):
    return lax.ppermute(value, "dp", [(0, 1), (1, 0)])


def to_all(block, axis, size):
    copies = jnp.broadcast_to(block[None], (size,) + block.shape)
    return lax.all_to_all(copies, axis, 0, 0, tiled=True)


def sum_along(pieces, axis):
    pieces = lax.all_to_all(pieces, axis, 0, 0, tiled=True)
    return jnp.sum(pieces.astype(jnp.float32), axis=0).astype(jnp.bfloat16)


def per_device(features, up_weight, out_grad):
    tokens, depth = features.shape
    half = up_weight.shape[1] // 2
    replica = lax.axis_index("dp")
    features = features.T

    def half_of(value, which):
        return lax.dynamic_slice_in_dim(value, which * half, half, axis=1)

    def by_replica(mine, other, axis):
        parts = jnp.where(replica == 0, mine, other), jnp.where(replica == 0, other, mine)
        return jnp.concatenate(parts, axis=axis)

    weight = lax.all_gather(half_of(up_weight, replica), "row", axis=0, tiled=True)
    line = to_all(features, ("dp", "y"), 2 * SIDE)
    by_depth = to_all(line, "x", SIDE)
    turns = [(r * COLS + c, c * COLS + r) for r in range(ROWS) for c in range(COLS)]
    turned = lax.ppermute(features, ("row",) + COL, turns)
    turned_line = to_all(after(turned, line), ("dp", "y"), 2 * SIDE)
    out_grad = by_replica(
        half_of(out_grad, replica), to_replica(half_of(out_grad, 1 - replica)), 0
    )

    hidden = hidden_sum(by_depth, weight)
    normal_cdf = 0.5 * (1.0 + jax.scipy.special.erf(hidden / math.sqrt(2.0)))
    density = jnp.exp(-0.5 * hidden * hidden) / math.sqrt(2.0 * math.pi)
    gelu_half = (hidden * normal_cdf).astype(jnp.bfloat16)
    hidden_grad = (out_grad.astype(jnp.float32) * (normal_cdf + hidden * density)).astype(
        jnp.bfloat16
    )
    grads = lax.all_gather(hidden_grad, "row", axis=0, tiled=True)

    by_token = to_all(after(turned_line, hidden_grad), "x", SIDE)
    pieces = input_grad_pieces(weight, after(hidden_grad, by_token))
    feature_grad = sum_along(sum_along(pieces, "x"), ("dp", "y")).T

    mine, other = (
        lax.dynamic_slice_in_dim(gelu_half, which * tokens, tokens, axis=0)
        for which in (replica, 1 - replica)
    )
    gelu_out = by_replica(mine, to_replica(other), 1)
    own = token_sum(by_token, grads)
    weight_grad = by_replica(own, to_replica(own), 1).astype(jnp.float32)
    return (gelu_out, feature_grad, weight_grad)


def solution(mesh):
    names = ("dp", "row") + COL
    fine = Mesh(mesh.devices.reshape(2, ROWS, SIDE, SIDE), names)
    by_tokens = P(("dp", "row"), COL)
    placed = (by_tokens, P("row", COL), by_tokens)
    return jax.shard_map(
        per_device,
        mesh=fine,
        in_specs=placed,
        out_specs=(by_tokens, by_tokens, P("row", COL)),
        check_vma=False,
    )
```

```python
import math

import jax
import jax.numpy as jnp
from jax import lax
from jax.experimental import pallas as pl
from jax.experimental.pallas import tpu as pltpu
from jax.sharding import Mesh
from jax.sharding import PartitionSpec as P

ROWS = 16
COLS = 16
SIDE = 4
LANES = 256
VMEM_BYTES = 32 * 2**20
TILED_VMEM_BYTES = 56 * 2**20
COL = ("y", "x")


def after(value, *others):
    return lax.optimization_barrier((value,) + others)[0]


def cost_of(flops, operands, out_shape):
    moved = sum(x.size * x.dtype.itemsize for x in (*operands, out_shape))
    return pl.CostEstimate(flops=flops, bytes_accessed=moved, transcendentals=0)


def tiled_kernel(kernel, out_shape, flops, blocks, value):
    whole = pl.BlockSpec(blocks.shape, lambda tile: (0,) * blocks.ndim)
    return pl.pallas_call(
        kernel,
        out_shape=out_shape,
        grid=(out_shape.shape[1] // LANES,),
        in_specs=[whole, pl.BlockSpec((value.shape[0], LANES), lambda tile: (0, tile))],
        out_specs=pl.BlockSpec((out_shape.shape[0], LANES), lambda tile: (0, tile)),
        compiler_params=pltpu.CompilerParams(vmem_limit_bytes=TILED_VMEM_BYTES),
        cost_estimate=cost_of(flops, (blocks, value), out_shape),
    )(blocks, value)


def both_replicas(block_ref, col):
    y, x = divmod(col, SIDE)
    return jnp.concatenate([block_ref[x, y], block_ref[x, SIDE + y]], axis=1)


def hidden_kernel(block_ref, weight_ref, hidden_ref):
    depth = block_ref.shape[2]
    total = None
    for col in range(COLS):
        term = lax.dot_general(
            both_replicas(block_ref, col),
            weight_ref[pl.ds(col * depth, depth), :],
            (((0,), (0,)), ((), ())),
            preferred_element_type=jnp.float32,
        )
        total = term if total is None else total + term
    hidden_ref[...] = total


def hidden_sum(blocks, weight):
    tokens = 2 * blocks.shape[3]
    out_shape = jax.ShapeDtypeStruct((tokens, weight.shape[1]), jnp.float32)
    return tiled_kernel(hidden_kernel, out_shape, 2 * tokens * weight.size, blocks, weight)


def input_grad_kernel(weight_ref, grad_ref, pieces_ref):
    depth, tokens = pieces_ref.shape[2:]
    for col in range(COLS):
        y, x = divmod(col, SIDE)
        piece = lax.dot_general(
            weight_ref[pl.ds(col * depth, depth), :],
            grad_ref[...],
            (((1,), (1,)), ((), ())),
            preferred_element_type=jnp.float32,
        ).astype(jnp.bfloat16)
        pieces_ref[x, y] = piece[:, :tokens]
        pieces_ref[x, SIDE + y] = piece[:, tokens:]


def input_grad_pieces(weight, grad):
    depth = weight.shape[0] // COLS
    out_shape = jax.ShapeDtypeStruct((SIDE, 2 * SIDE, depth, grad.shape[0] // 2), jnp.bfloat16)
    return pl.pallas_call(
        input_grad_kernel,
        out_shape=out_shape,
        in_specs=[pl.BlockSpec(memory_space=pltpu.VMEM)] * 2,
        out_specs=pl.BlockSpec(memory_space=pltpu.VMEM),
        compiler_params=pltpu.CompilerParams(vmem_limit_bytes=VMEM_BYTES),
        cost_estimate=cost_of(2 * weight.size * grad.shape[0], (weight, grad), out_shape),
    )(weight, grad)


def token_sum_kernel(block_ref, grad_ref, total_ref):
    tokens = 2 * block_ref.shape[3]
    total = None
    for row in range(ROWS):
        term = jnp.dot(
            both_replicas(block_ref, row),
            grad_ref[pl.ds(row * tokens, tokens), :],
            preferred_element_type=jnp.float32,
        )
        total = term if total is None else total + term
    total_ref[...] = total.astype(total_ref.dtype)


def token_sum(blocks, grads):
    depth = blocks.shape[2]
    out_shape = jax.ShapeDtypeStruct((depth, grads.shape[1]), jnp.bfloat16)
    return tiled_kernel(token_sum_kernel, out_shape, 2 * depth * grads.size, blocks, grads)


def to_replica(value):
    return lax.ppermute(value, "dp", [(0, 1), (1, 0)])


def to_all(block, axis, size):
    copies = jnp.broadcast_to(block[None], (size,) + block.shape)
    return lax.all_to_all(copies, axis, 0, 0, tiled=True)


def sum_along(pieces, axis):
    pieces = lax.all_to_all(pieces, axis, 0, 0, tiled=True)
    return jnp.sum(pieces.astype(jnp.float32), axis=0).astype(jnp.bfloat16)


def per_device(features, up_weight, out_grad):
    tokens, depth = features.shape
    half = up_weight.shape[1] // 2
    replica = lax.axis_index("dp")
    features = features.T

    def half_of(value, which):
        return lax.dynamic_slice_in_dim(value, which * half, half, axis=1)

    def by_replica(mine, other, axis):
        parts = jnp.where(replica == 0, mine, other), jnp.where(replica == 0, other, mine)
        return jnp.concatenate(parts, axis=axis)

    weight = lax.all_gather(half_of(up_weight, replica), "row", axis=0, tiled=True)
    line = to_all(features, ("dp", "y"), 2 * SIDE)
    by_depth = to_all(line, "x", SIDE)
    turns = [(r * COLS + c, c * COLS + r) for r in range(ROWS) for c in range(COLS)]
    turned = lax.ppermute(features, ("row",) + COL, turns)
    turned_line = to_all(after(turned, line), ("dp", "y"), 2 * SIDE)
    out_grad = by_replica(
        half_of(out_grad, replica), to_replica(half_of(out_grad, 1 - replica)), 0
    )

    hidden = hidden_sum(after(by_depth, turned_line), weight)
    normal_cdf = 0.5 * (1.0 + jax.scipy.special.erf(hidden / math.sqrt(2.0)))
    density = jnp.exp(-0.5 * hidden * hidden) / math.sqrt(2.0 * math.pi)
    gelu_half = (hidden * normal_cdf).astype(jnp.bfloat16)
    hidden_grad = (out_grad.astype(jnp.float32) * (normal_cdf + hidden * density)).astype(
        jnp.bfloat16
    )
    grads = lax.all_gather(hidden_grad, "row", axis=0, tiled=True)

    by_token = to_all(after(turned_line, hidden_grad), "x", SIDE)
    pieces = input_grad_pieces(weight, hidden_grad)
    own = token_sum(by_token, grads)
    feature_grad = sum_along(after(sum_along(pieces, "x"), own), ("dp", "y")).T

    mine, other = (
        lax.dynamic_slice_in_dim(gelu_half, which * tokens, tokens, axis=0)
        for which in (replica, 1 - replica)
    )
    gelu_out = by_replica(mine, to_replica(other), 1)
    weight_grad = by_replica(own, to_replica(own), 1).astype(jnp.float32)
    return (gelu_out, feature_grad, weight_grad)


def solution(mesh):
    names = ("dp", "row") + COL
    fine = Mesh(mesh.devices.reshape(2, ROWS, SIDE, SIDE), names)
    by_tokens = P(("dp", "row"), COL)
    placed = (by_tokens, P("row", COL), by_tokens)
    return jax.shard_map(
        per_device,
        mesh=fine,
        in_specs=placed,
        out_specs=(by_tokens, by_tokens, P("row", COL)),
        check_vma=False,
    )
```

```python
import math

import jax
import jax.numpy as jnp
from jax import lax
from jax.experimental import pallas as pl
from jax.experimental.pallas import tpu as pltpu
from jax.sharding import Mesh
from jax.sharding import PartitionSpec as P

ROWS = 16
COLS = 16
SIDE = 4
LANES = 256
VMEM_BYTES = 32 * 2**20
COL = ("y", "x")


def after(value, *others):
    return lax.optimization_barrier((value,) + others)[0]


def local_kernel(kernel, out_shape, flops, operands):
    moved = sum(x.size * x.dtype.itemsize for x in (*operands, out_shape))
    return pl.pallas_call(
        kernel,
        out_shape=out_shape,
        in_specs=[pl.BlockSpec(memory_space=pltpu.VMEM)] * len(operands),
        out_specs=pl.BlockSpec(memory_space=pltpu.VMEM),
        compiler_params=pltpu.CompilerParams(vmem_limit_bytes=VMEM_BYTES),
        cost_estimate=pl.CostEstimate(flops=flops, bytes_accessed=moved, transcendentals=0),
    )(*operands)


def both_replicas(block_ref, col):
    y, x = divmod(col, SIDE)
    return jnp.concatenate([block_ref[x, y], block_ref[x, SIDE + y]], axis=1)


def hidden_kernel(block_ref, weight_ref, hidden_ref):
    depth = block_ref.shape[2]
    blocks = [both_replicas(block_ref, col) for col in range(COLS)]
    for start in range(0, hidden_ref.shape[1], LANES):
        units = pl.ds(start, LANES)
        total = None
        for col, block in enumerate(blocks):
            term = lax.dot_general(
                block,
                weight_ref[pl.ds(col * depth, depth), units],
                (((0,), (0,)), ((), ())),
                preferred_element_type=jnp.float32,
            )
            total = term if total is None else total + term
        hidden_ref[:, units] = total


def hidden_sum(blocks, weight):
    tokens = 2 * blocks.shape[3]
    out_shape = jax.ShapeDtypeStruct((tokens, weight.shape[1]), jnp.float32)
    return local_kernel(hidden_kernel, out_shape, 2 * tokens * weight.size, (blocks, weight))


def input_grad_kernel(weight_ref, grad_ref, pieces_ref):
    depth, tokens = pieces_ref.shape[2:]
    for col in range(COLS):
        y, x = divmod(col, SIDE)
        piece = lax.dot_general(
            weight_ref[pl.ds(col * depth, depth), :],
            grad_ref[...],
            (((1,), (1,)), ((), ())),
            preferred_element_type=jnp.float32,
        ).astype(jnp.bfloat16)
        pieces_ref[x, y] = piece[:, :tokens]
        pieces_ref[x, SIDE + y] = piece[:, tokens:]


def input_grad_pieces(weight, grad):
    depth = weight.shape[0] // COLS
    out_shape = jax.ShapeDtypeStruct((SIDE, 2 * SIDE, depth, grad.shape[0] // 2), jnp.bfloat16)
    return local_kernel(input_grad_kernel, out_shape, 2 * weight.size * grad.shape[0], (weight, grad))


def token_sum_kernel(block_ref, grad_ref, total_ref):
    tokens = 2 * block_ref.shape[3]
    blocks = [both_replicas(block_ref, row) for row in range(ROWS)]
    for start in range(0, total_ref.shape[1], LANES):
        units = pl.ds(start, LANES)
        total = None
        for row, block in enumerate(blocks):
            term = jnp.dot(
                block,
                grad_ref[pl.ds(row * tokens, tokens), units],
                preferred_element_type=jnp.float32,
            )
            total = term if total is None else total + term
        total_ref[:, units] = total.astype(total_ref.dtype)


def token_sum(blocks, grads):
    depth = blocks.shape[2]
    out_shape = jax.ShapeDtypeStruct((depth, grads.shape[1]), jnp.bfloat16)
    return local_kernel(token_sum_kernel, out_shape, 2 * depth * grads.size, (blocks, grads))


def to_replica(value):
    return lax.ppermute(value, "dp", [(0, 1), (1, 0)])


def to_all(block, axis, size):
    copies = jnp.broadcast_to(block[None], (size,) + block.shape)
    return lax.all_to_all(copies, axis, 0, 0, tiled=True)


def sum_along(pieces, axis):
    pieces = lax.all_to_all(pieces, axis, 0, 0, tiled=True)
    return jnp.sum(pieces.astype(jnp.float32), axis=0).astype(jnp.bfloat16)


def per_device(features, up_weight, out_grad):
    tokens, depth = features.shape
    half = up_weight.shape[1] // 2
    replica = lax.axis_index("dp")
    features = features.T

    def half_of(value, which):
        return lax.dynamic_slice_in_dim(value, which * half, half, axis=1)

    def by_replica(mine, other, axis):
        parts = jnp.where(replica == 0, mine, other), jnp.where(replica == 0, other, mine)
        return jnp.concatenate(parts, axis=axis)

    weight = lax.all_gather(half_of(up_weight, replica), "row", axis=0, tiled=True)
    line = to_all(features, ("dp", "y"), 2 * SIDE)
    by_depth = to_all(line, "x", SIDE)
    turns = [(r * COLS + c, c * COLS + r) for r in range(ROWS) for c in range(COLS)]
    turned = lax.ppermute(features, ("row",) + COL, turns)
    out_grad = by_replica(
        half_of(out_grad, replica), to_replica(half_of(out_grad, 1 - replica)), 0
    )

    hidden = hidden_sum(after(by_depth, turned), weight)
    normal_cdf = 0.5 * (1.0 + jax.scipy.special.erf(hidden / math.sqrt(2.0)))
    density = jnp.exp(-0.5 * hidden * hidden) / math.sqrt(2.0 * math.pi)
    gelu_half = (hidden * normal_cdf).astype(jnp.bfloat16)
    hidden_grad = (out_grad.astype(jnp.float32) * (normal_cdf + hidden * density)).astype(
        jnp.bfloat16
    )
    grads = lax.all_gather(hidden_grad, "row", axis=0, tiled=True)

    by_token = to_all(after(turned, hidden_grad), ("dp", "y"), 2 * SIDE)
    by_token = to_all(by_token, "x", SIDE)
    pieces = input_grad_pieces(weight, hidden_grad)
    own = token_sum(by_token, grads)
    feature_grad = sum_along(sum_along(pieces, "x"), ("dp", "y")).T

    mine, other = (
        lax.dynamic_slice_in_dim(gelu_half, which * tokens, tokens, axis=0)
        for which in (replica, 1 - replica)
    )
    gelu_out = by_replica(mine, to_replica(other), 1)
    weight_grad = by_replica(own, to_replica(own), 1).astype(jnp.float32)
    return (gelu_out, feature_grad, weight_grad)


def solution(mesh):
    names = ("dp", "row") + COL
    fine = Mesh(mesh.devices.reshape(2, ROWS, SIDE, SIDE), names)
    by_tokens = P(("dp", "row"), COL)
    placed = (by_tokens, P("row", COL), by_tokens)
    return jax.shard_map(
        per_device,
        mesh=fine,
        in_specs=placed,
        out_specs=(by_tokens, by_tokens, P("row", COL)),
        check_vma=False,
    )
```

```python
import math

import jax
import jax.numpy as jnp
from jax import lax
from jax.experimental import pallas as pl
from jax.experimental.pallas import tpu as pltpu
from jax.sharding import Mesh
from jax.sharding import PartitionSpec as P

ROWS = 16
COLS = 16
SIDE = 4
LANES = 256
VMEM_BYTES = 32 * 2**20
COL = ("y", "x")


def after(value, *others):
    return lax.optimization_barrier((value,) + others)[0]


def local_kernel(kernel, out_shape, flops, operands):
    moved = sum(x.size * x.dtype.itemsize for x in (*operands, out_shape))
    return pl.pallas_call(
        kernel,
        out_shape=out_shape,
        in_specs=[pl.BlockSpec(memory_space=pltpu.VMEM)] * len(operands),
        out_specs=pl.BlockSpec(memory_space=pltpu.VMEM),
        compiler_params=pltpu.CompilerParams(vmem_limit_bytes=VMEM_BYTES),
        cost_estimate=pl.CostEstimate(flops=flops, bytes_accessed=moved, transcendentals=0),
    )(*operands)


def both_replicas(block_ref, col):
    y, x = divmod(col, SIDE)
    return jnp.concatenate([block_ref[x, y], block_ref[x, SIDE + y]], axis=1)


def hidden_kernel(block_ref, weight_ref, hidden_ref):
    depth = block_ref.shape[2]
    blocks = [both_replicas(block_ref, col) for col in range(COLS)]
    for start in range(0, hidden_ref.shape[1], LANES):
        units = pl.ds(start, LANES)
        total = None
        for col, block in enumerate(blocks):
            term = lax.dot_general(
                block,
                weight_ref[pl.ds(col * depth, depth), units],
                (((0,), (0,)), ((), ())),
                preferred_element_type=jnp.float32,
            )
            total = term if total is None else total + term
        hidden_ref[:, units] = total


def hidden_sum(blocks, weight):
    tokens = 2 * blocks.shape[3]
    out_shape = jax.ShapeDtypeStruct((tokens, weight.shape[1]), jnp.float32)
    return local_kernel(hidden_kernel, out_shape, 2 * tokens * weight.size, (blocks, weight))


def input_grad_kernel(weight_ref, grad_ref, pieces_ref):
    depth, tokens = pieces_ref.shape[2:]
    for col in range(COLS):
        y, x = divmod(col, SIDE)
        piece = lax.dot_general(
            weight_ref[pl.ds(col * depth, depth), :],
            grad_ref[...],
            (((1,), (1,)), ((), ())),
            preferred_element_type=jnp.float32,
        ).astype(jnp.bfloat16)
        pieces_ref[x, y] = piece[:, :tokens]
        pieces_ref[x, SIDE + y] = piece[:, tokens:]


def input_grad_pieces(weight, grad):
    depth = weight.shape[0] // COLS
    out_shape = jax.ShapeDtypeStruct((SIDE, 2 * SIDE, depth, grad.shape[0] // 2), jnp.bfloat16)
    return local_kernel(input_grad_kernel, out_shape, 2 * weight.size * grad.shape[0], (weight, grad))


def token_sum_kernel(block_ref, grad_ref, total_ref):
    tokens = 2 * block_ref.shape[3]
    blocks = [both_replicas(block_ref, row) for row in range(ROWS)]
    for start in range(0, total_ref.shape[1], LANES):
        units = pl.ds(start, LANES)
        total = None
        for row, block in enumerate(blocks):
            term = jnp.dot(
                block,
                grad_ref[pl.ds(row * tokens, tokens), units],
                preferred_element_type=jnp.float32,
            )
            total = term if total is None else total + term
        total_ref[:, units] = total.astype(total_ref.dtype)


def token_sum(blocks, grads):
    depth = blocks.shape[2]
    out_shape = jax.ShapeDtypeStruct((depth, grads.shape[1]), jnp.bfloat16)
    return local_kernel(token_sum_kernel, out_shape, 2 * depth * grads.size, (blocks, grads))


def to_replica(value):
    return lax.ppermute(value, "dp", [(0, 1), (1, 0)])


def to_all(block, axis, size):
    copies = jnp.broadcast_to(block[None], (size,) + block.shape)
    return lax.all_to_all(copies, axis, 0, 0, tiled=True)


def sum_along(pieces, axis):
    pieces = lax.all_to_all(pieces, axis, 0, 0, tiled=True)
    return jnp.sum(pieces.astype(jnp.float32), axis=0).astype(jnp.bfloat16)


def per_device(features, up_weight, out_grad):
    tokens, depth = features.shape
    half = up_weight.shape[1] // 2
    replica = lax.axis_index("dp")
    features = features.T

    def half_of(value, which):
        return lax.dynamic_slice_in_dim(value, which * half, half, axis=1)

    def by_replica(mine, other, axis):
        parts = jnp.where(replica == 0, mine, other), jnp.where(replica == 0, other, mine)
        return jnp.concatenate(parts, axis=axis)

    weight = lax.all_gather(half_of(up_weight, replica), "row", axis=0, tiled=True)
    turns = [(r * COLS + c, c * COLS + r) for r in range(ROWS) for c in range(COLS)]
    turned = lax.ppermute(features, ("row",) + COL, turns)
    lines = to_all(jnp.stack([features, turned]), ("dp", "y"), 2 * SIDE)
    by_depth = to_all(lines[:, 0], "x", SIDE)
    out_grad = by_replica(
        half_of(out_grad, replica), to_replica(half_of(out_grad, 1 - replica)), 0
    )

    hidden = hidden_sum(by_depth, weight)
    normal_cdf = 0.5 * (1.0 + jax.scipy.special.erf(hidden / math.sqrt(2.0)))
    density = jnp.exp(-0.5 * hidden * hidden) / math.sqrt(2.0 * math.pi)
    gelu_half = (hidden * normal_cdf).astype(jnp.bfloat16)
    hidden_grad = (out_grad.astype(jnp.float32) * (normal_cdf + hidden * density)).astype(
        jnp.bfloat16
    )
    grads = lax.all_gather(hidden_grad, "row", axis=0, tiled=True)

    by_token = to_all(after(lines[:, 1], hidden_grad), "x", SIDE)
    pieces = input_grad_pieces(weight, hidden_grad)
    own = token_sum(by_token, grads)
    feature_grad = sum_along(after(sum_along(pieces, "x"), own), ("dp", "y")).T

    mine, other = (
        lax.dynamic_slice_in_dim(gelu_half, which * tokens, tokens, axis=0)
        for which in (replica, 1 - replica)
    )
    gelu_out = by_replica(mine, to_replica(other), 1)
    weight_grad = by_replica(own, to_replica(own), 1).astype(jnp.float32)
    return (gelu_out, feature_grad, weight_grad)


def solution(mesh):
    names = ("dp", "row") + COL
    fine = Mesh(mesh.devices.reshape(2, ROWS, SIDE, SIDE), names)
    by_tokens = P(("dp", "row"), COL)
    placed = (by_tokens, P("row", COL), by_tokens)
    return jax.shard_map(
        per_device,
        mesh=fine,
        in_specs=placed,
        out_specs=(by_tokens, by_tokens, P("row", COL)),
        check_vma=False,
    )
```

```python
import math

import jax
import jax.numpy as jnp
from jax import lax
from jax.experimental import pallas as pl
from jax.experimental.pallas import tpu as pltpu
from jax.sharding import Mesh
from jax.sharding import PartitionSpec as P

ROWS = 16
COLS = 16
SIDE = 4
LANES = 256
VMEM_BYTES = 32 * 2**20
COL = ("y", "x")


def after(value, *others):
    return lax.optimization_barrier((value,) + others)[0]


def local_kernel(kernel, out_shape, flops, operands, place=None):
    moved = sum(x.size * x.dtype.itemsize for x in (*operands, out_shape))
    in_specs = [pl.BlockSpec(memory_space=pltpu.VMEM)] * len(operands)
    if place is not None:
        in_specs = [pl.BlockSpec(memory_space=pltpu.SMEM)] + in_specs
        operands = (place, *operands)
    return pl.pallas_call(
        kernel,
        out_shape=out_shape,
        in_specs=in_specs,
        out_specs=pl.BlockSpec(memory_space=pltpu.VMEM),
        compiler_params=pltpu.CompilerParams(vmem_limit_bytes=VMEM_BYTES),
        cost_estimate=pl.CostEstimate(flops=flops, bytes_accessed=moved, transcendentals=0),
    )(*operands)


def both_replicas(block_ref, col):
    y, x = divmod(col, SIDE)
    return jnp.concatenate([block_ref[x, y], block_ref[x, SIDE + y]], axis=1)


def hidden_kernel(block_ref, weight_ref, hidden_ref):
    depth = block_ref.shape[2]
    blocks = [both_replicas(block_ref, col) for col in range(COLS)]
    for start in range(0, hidden_ref.shape[1], LANES):
        units = pl.ds(start, LANES)
        total = None
        for col, block in enumerate(blocks):
            term = lax.dot_general(
                block,
                weight_ref[pl.ds(col * depth, depth), units],
                (((0,), (0,)), ((), ())),
                preferred_element_type=jnp.float32,
            )
            total = term if total is None else total + term
        hidden_ref[:, units] = total


def hidden_sum(blocks, weight):
    tokens = 2 * blocks.shape[3]
    out_shape = jax.ShapeDtypeStruct((tokens, weight.shape[1]), jnp.float32)
    return local_kernel(hidden_kernel, out_shape, 2 * tokens * weight.size, (blocks, weight))


def input_grad_kernel(weight_ref, grad_ref, pieces_ref):
    depth, tokens = pieces_ref.shape[2:]
    for col in range(COLS):
        y, x = divmod(col, SIDE)
        piece = lax.dot_general(
            weight_ref[pl.ds(col * depth, depth), :],
            grad_ref[...],
            (((1,), (1,)), ((), ())),
            preferred_element_type=jnp.float32,
        ).astype(jnp.bfloat16)
        pieces_ref[x, y] = piece[:, :tokens]
        pieces_ref[x, SIDE + y] = piece[:, tokens:]


def input_grad_pieces(weight, grad):
    depth = weight.shape[0] // COLS
    out_shape = jax.ShapeDtypeStruct((SIDE, 2 * SIDE, depth, grad.shape[0] // 2), jnp.bfloat16)
    return local_kernel(input_grad_kernel, out_shape, 2 * weight.size * grad.shape[0], (weight, grad))


def token_sum_kernel(place_ref, block_ref, grad_ref, total_ref):
    tokens = 2 * block_ref.shape[2]
    blocks = []
    for row in range(ROWS):
        parts = [block_ref[place_ref[2 * row + d]] for d in range(2)]
        blocks.append(jnp.concatenate(parts, axis=1))
    for start in range(0, total_ref.shape[1], LANES):
        units = pl.ds(start, LANES)
        total = None
        for row, block in enumerate(blocks):
            term = jnp.dot(
                block,
                grad_ref[pl.ds(row * tokens, tokens), units],
                preferred_element_type=jnp.float32,
            )
            total = term if total is None else total + term
        total_ref[:, units] = total.astype(total_ref.dtype)


def token_sum(place, blocks, grads):
    depth = blocks.shape[1]
    out_shape = jax.ShapeDtypeStruct((depth, grads.shape[1]), jnp.bfloat16)
    return local_kernel(
        token_sum_kernel, out_shape, 2 * depth * grads.size, (blocks, grads), place
    )


def places():
    tables = []
    for replica in range(2):
        for col in range(COLS):
            y, x = divmod(col, SIDE)
            tables.append(
                [
                    ((x - c) % SIDE * SIDE + (y - c // SIDE) % SIDE) * 2 + (replica ^ d)
                    for c in range(COLS)
                    for d in range(2)
                ]
            )
    return jnp.array(tables, jnp.int32)[lax.axis_index(("dp",) + COL)]


def shifted(value, axis, steps):
    return lax.ppermute(value, axis, [(i, (i + steps) % SIDE) for i in range(SIDE)])


def from_line(block):
    pair = jnp.stack([block, to_replica(block)])
    return jnp.concatenate([pair] + [shifted(pair, "y", d) for d in range(1, SIDE)])


def from_lines(line):
    return jnp.concatenate([line] + [shifted(line, "x", e) for e in range(1, SIDE)])


def to_replica(value):
    return lax.ppermute(value, "dp", [(0, 1), (1, 0)])


def to_all(block, axis, size):
    copies = jnp.broadcast_to(block[None], (size,) + block.shape)
    return lax.all_to_all(copies, axis, 0, 0, tiled=True)


def sum_along(pieces, axis):
    pieces = lax.all_to_all(pieces, axis, 0, 0, tiled=True)
    return jnp.sum(pieces.astype(jnp.float32), axis=0).astype(jnp.bfloat16)


def per_device(features, up_weight, out_grad):
    tokens, depth = features.shape
    half = up_weight.shape[1] // 2
    replica = lax.axis_index("dp")
    features = features.T

    def half_of(value, which):
        return lax.dynamic_slice_in_dim(value, which * half, half, axis=1)

    def by_replica(mine, other, axis):
        parts = jnp.where(replica == 0, mine, other), jnp.where(replica == 0, other, mine)
        return jnp.concatenate(parts, axis=axis)

    weight = lax.all_gather(half_of(up_weight, replica), "row", axis=0, tiled=True)
    turns = [(r * COLS + c, c * COLS + r) for r in range(ROWS) for c in range(COLS)]
    turned = lax.ppermute(features, ("row",) + COL, turns)
    depth_line = to_all(features, ("dp", "y"), 2 * SIDE)
    by_depth = to_all(depth_line, "x", SIDE)
    token_line = from_line(after(turned, depth_line))
    out_grad = by_replica(
        half_of(out_grad, replica), to_replica(half_of(out_grad, 1 - replica)), 0
    )

    hidden = hidden_sum(after(by_depth, token_line), weight)
    normal_cdf = 0.5 * (1.0 + jax.scipy.special.erf(hidden / math.sqrt(2.0)))
    density = jnp.exp(-0.5 * hidden * hidden) / math.sqrt(2.0 * math.pi)
    gelu_half = (hidden * normal_cdf).astype(jnp.bfloat16)
    hidden_grad = (out_grad.astype(jnp.float32) * (normal_cdf + hidden * density)).astype(
        jnp.bfloat16
    )
    grads = lax.all_gather(hidden_grad, "row", axis=0, tiled=True)

    by_token = from_lines(after(token_line, hidden_grad))
    pieces = input_grad_pieces(weight, hidden_grad)
    own = token_sum(places(), by_token, grads)
    feature_grad = sum_along(sum_along(pieces, "x"), ("dp", "y")).T

    mine, other = (
        lax.dynamic_slice_in_dim(gelu_half, which * tokens, tokens, axis=0)
        for which in (replica, 1 - replica)
    )
    gelu_out = by_replica(mine, to_replica(other), 1)
    weight_grad = by_replica(own, to_replica(own), 1).astype(jnp.float32)
    return (gelu_out, feature_grad, weight_grad)


def solution(mesh):
    names = ("dp", "row") + COL
    fine = Mesh(mesh.devices.reshape(2, ROWS, SIDE, SIDE), names)
    by_tokens = P(("dp", "row"), COL)
    placed = (by_tokens, P("row", COL), by_tokens)
    return jax.shard_map(
        per_device,
        mesh=fine,
        in_specs=placed,
        out_specs=(by_tokens, by_tokens, P("row", COL)),
        check_vma=False,
    )
```

```python
import math

import jax
import jax.numpy as jnp
from jax import lax
from jax.experimental import pallas as pl
from jax.experimental.pallas import tpu as pltpu
from jax.sharding import Mesh
from jax.sharding import PartitionSpec as P

ROWS = 16
COLS = 16
SIDE = 4
LANES = 256
VMEM_BYTES = 32 * 2**20
COL = ("y", "x")


def after(value, *others):
    return lax.optimization_barrier((value,) + others)[0]


def local_kernel(kernel, out_shape, flops, operands, place=None):
    moved = sum(x.size * x.dtype.itemsize for x in (*operands, out_shape))
    in_specs = [pl.BlockSpec(memory_space=pltpu.VMEM)] * len(operands)
    if place is not None:
        in_specs = [pl.BlockSpec(memory_space=pltpu.SMEM)] + in_specs
        operands = (place, *operands)
    return pl.pallas_call(
        kernel,
        out_shape=out_shape,
        in_specs=in_specs,
        out_specs=pl.BlockSpec(memory_space=pltpu.VMEM),
        compiler_params=pltpu.CompilerParams(vmem_limit_bytes=VMEM_BYTES),
        cost_estimate=pl.CostEstimate(flops=flops, bytes_accessed=moved, transcendentals=0),
    )(*operands)


def both_replicas(block_ref, col):
    y, x = divmod(col, SIDE)
    return jnp.concatenate([block_ref[x, y], block_ref[x, SIDE + y]], axis=1)


def hidden_kernel(block_ref, weight_ref, hidden_ref):
    depth = block_ref.shape[2]
    blocks = [both_replicas(block_ref, col) for col in range(COLS)]
    for start in range(0, hidden_ref.shape[1], LANES):
        units = pl.ds(start, LANES)
        total = None
        for col, block in enumerate(blocks):
            term = lax.dot_general(
                block,
                weight_ref[pl.ds(col * depth, depth), units],
                (((0,), (0,)), ((), ())),
                preferred_element_type=jnp.float32,
            )
            total = term if total is None else total + term
        hidden_ref[:, units] = total


def hidden_sum(blocks, weight):
    tokens = 2 * blocks.shape[3]
    out_shape = jax.ShapeDtypeStruct((tokens, weight.shape[1]), jnp.float32)
    return local_kernel(hidden_kernel, out_shape, 2 * tokens * weight.size, (blocks, weight))


def input_grad_kernel(weight_ref, grad_ref, pieces_ref):
    depth, tokens = pieces_ref.shape[2:]
    for col in range(COLS):
        y, x = divmod(col, SIDE)
        piece = lax.dot_general(
            weight_ref[pl.ds(col * depth, depth), :],
            grad_ref[...],
            (((1,), (1,)), ((), ())),
            preferred_element_type=jnp.float32,
        ).astype(jnp.bfloat16)
        pieces_ref[x, y] = piece[:, :tokens]
        pieces_ref[x, SIDE + y] = piece[:, tokens:]


def input_grad_pieces(weight, grad):
    depth = weight.shape[0] // COLS
    out_shape = jax.ShapeDtypeStruct((SIDE, 2 * SIDE, depth, grad.shape[0] // 2), jnp.bfloat16)
    return local_kernel(input_grad_kernel, out_shape, 2 * weight.size * grad.shape[0], (weight, grad))


def token_sum_kernel(place_ref, block_ref, grad_ref, total_ref):
    tokens = 2 * block_ref.shape[2]
    blocks = []
    for row in range(ROWS):
        parts = [block_ref[place_ref[2 * row + d]] for d in range(2)]
        blocks.append(jnp.concatenate(parts, axis=1))
    for start in range(0, total_ref.shape[1], LANES):
        units = pl.ds(start, LANES)
        total = None
        for row, block in enumerate(blocks):
            term = jnp.dot(
                block,
                grad_ref[pl.ds(row * tokens, tokens), units],
                preferred_element_type=jnp.float32,
            )
            total = term if total is None else total + term
        total_ref[:, units] = total.astype(total_ref.dtype)


def token_sum(place, blocks, grads):
    depth = blocks.shape[1]
    out_shape = jax.ShapeDtypeStruct((depth, grads.shape[1]), jnp.bfloat16)
    return local_kernel(
        token_sum_kernel, out_shape, 2 * depth * grads.size, (blocks, grads), place
    )


def places():
    tables = []
    for replica in range(2):
        for col in range(COLS):
            y, x = divmod(col, SIDE)
            tables.append(
                [
                    ((x - c) % SIDE * SIDE + (y - c // SIDE) % SIDE) * 2 + (replica ^ d)
                    for c in range(COLS)
                    for d in range(2)
                ]
            )
    return jnp.array(tables, jnp.int32)[lax.axis_index(("dp",) + COL)]


def shifted(value, axis, steps):
    return lax.ppermute(value, axis, [(i, (i + steps) % SIDE) for i in range(SIDE)])


def from_line(block):
    pair = jnp.stack([block, to_replica(block)])
    return jnp.concatenate([pair] + [shifted(pair, "y", d) for d in range(1, SIDE)])


def from_lines(line):
    return jnp.concatenate([line] + [shifted(line, "x", e) for e in range(1, SIDE)])


def to_replica(value):
    return lax.ppermute(value, "dp", [(0, 1), (1, 0)])


def to_all(block, axis, size):
    copies = jnp.broadcast_to(block[None], (size,) + block.shape)
    return lax.all_to_all(copies, axis, 0, 0, tiled=True)


def sum_along(pieces, axis):
    pieces = lax.all_to_all(pieces, axis, 0, 0, tiled=True)
    return jnp.sum(pieces.astype(jnp.float32), axis=0).astype(jnp.bfloat16)


def per_device(features, up_weight, out_grad):
    tokens, depth = features.shape
    half = up_weight.shape[1] // 2
    replica = lax.axis_index("dp")
    features = features.T

    def half_of(value, which):
        return lax.dynamic_slice_in_dim(value, which * half, half, axis=1)

    def by_replica(mine, other, axis):
        parts = jnp.where(replica == 0, mine, other), jnp.where(replica == 0, other, mine)
        return jnp.concatenate(parts, axis=axis)

    weight = lax.all_gather(half_of(up_weight, replica), "row", axis=0, tiled=True)
    turns = [(r * COLS + c, c * COLS + r) for r in range(ROWS) for c in range(COLS)]
    turned = lax.ppermute(features, ("row",) + COL, turns)
    depth_line = to_all(features, ("dp", "y"), 2 * SIDE)
    by_depth = to_all(depth_line, "x", SIDE)
    out_grad = by_replica(
        half_of(out_grad, replica), to_replica(half_of(out_grad, 1 - replica)), 0
    )

    hidden = hidden_sum(after(by_depth, turned), weight)
    normal_cdf = 0.5 * (1.0 + jax.scipy.special.erf(hidden / math.sqrt(2.0)))
    density = jnp.exp(-0.5 * hidden * hidden) / math.sqrt(2.0 * math.pi)
    gelu_half = (hidden * normal_cdf).astype(jnp.bfloat16)
    hidden_grad = (out_grad.astype(jnp.float32) * (normal_cdf + hidden * density)).astype(
        jnp.bfloat16
    )
    grads = lax.all_gather(hidden_grad, "row", axis=0, tiled=True)

    by_token = from_lines(from_line(after(turned, hidden_grad)))
    pieces = input_grad_pieces(weight, hidden_grad)
    own = token_sum(places(), by_token, grads)
    feature_grad = sum_along(sum_along(pieces, "x"), ("dp", "y")).T

    mine, other = (
        lax.dynamic_slice_in_dim(gelu_half, which * tokens, tokens, axis=0)
        for which in (replica, 1 - replica)
    )
    gelu_out = by_replica(mine, to_replica(other), 1)
    weight_grad = by_replica(own, to_replica(own), 1).astype(jnp.float32)
    return (gelu_out, feature_grad, weight_grad)


def solution(mesh):
    names = ("dp", "row") + COL
    fine = Mesh(mesh.devices.reshape(2, ROWS, SIDE, SIDE), names)
    by_tokens = P(("dp", "row"), COL)
    placed = (by_tokens, P("row", COL), by_tokens)
    return jax.shard_map(
        per_device,
        mesh=fine,
        in_specs=placed,
        out_specs=(by_tokens, by_tokens, P("row", COL)),
        check_vma=False,
    )
```

```python
import math

import jax
import jax.numpy as jnp
from jax import lax
from jax.experimental import pallas as pl
from jax.experimental.pallas import tpu as pltpu
from jax.sharding import Mesh
from jax.sharding import PartitionSpec as P

ROWS = 16
COLS = 16
SIDE = 4
LANES = 256
VMEM_BYTES = 32 * 2**20
COL = ("y", "x")


def after(value, *others):
    return lax.optimization_barrier((value,) + others)[0]


def local_kernel(kernel, out_shape, flops, operands, place=None):
    moved = sum(x.size * x.dtype.itemsize for x in (*operands, out_shape))
    in_specs = [pl.BlockSpec(memory_space=pltpu.VMEM)] * len(operands)
    if place is not None:
        in_specs = [pl.BlockSpec(memory_space=pltpu.SMEM)] + in_specs
        operands = (place, *operands)
    return pl.pallas_call(
        kernel,
        out_shape=out_shape,
        in_specs=in_specs,
        out_specs=pl.BlockSpec(memory_space=pltpu.VMEM),
        compiler_params=pltpu.CompilerParams(vmem_limit_bytes=VMEM_BYTES),
        cost_estimate=pl.CostEstimate(flops=flops, bytes_accessed=moved, transcendentals=0),
    )(*operands)


def both_replicas(block_ref, col):
    y, x = divmod(col, SIDE)
    return jnp.concatenate([block_ref[x, y], block_ref[x, SIDE + y]], axis=1)


def hidden_kernel(block_ref, weight_ref, hidden_ref):
    depth = block_ref.shape[2]
    blocks = [both_replicas(block_ref, col) for col in range(COLS)]
    for start in range(0, hidden_ref.shape[1], LANES):
        units = pl.ds(start, LANES)
        total = None
        for col, block in enumerate(blocks):
            term = lax.dot_general(
                block,
                weight_ref[pl.ds(col * depth, depth), units],
                (((0,), (0,)), ((), ())),
                preferred_element_type=jnp.float32,
            )
            total = term if total is None else total + term
        hidden_ref[:, units] = total


def hidden_sum(blocks, weight):
    tokens = 2 * blocks.shape[3]
    out_shape = jax.ShapeDtypeStruct((tokens, weight.shape[1]), jnp.float32)
    return local_kernel(hidden_kernel, out_shape, 2 * tokens * weight.size, (blocks, weight))


def input_grad_kernel(weight_ref, grad_ref, pieces_ref):
    depth, tokens = pieces_ref.shape[2:]
    for col in range(COLS):
        y, x = divmod(col, SIDE)
        piece = lax.dot_general(
            weight_ref[pl.ds(col * depth, depth), :],
            grad_ref[...],
            (((1,), (1,)), ((), ())),
            preferred_element_type=jnp.float32,
        ).astype(jnp.bfloat16)
        pieces_ref[x, y] = piece[:, :tokens]
        pieces_ref[x, SIDE + y] = piece[:, tokens:]


def input_grad_pieces(weight, grad):
    depth = weight.shape[0] // COLS
    out_shape = jax.ShapeDtypeStruct((SIDE, 2 * SIDE, depth, grad.shape[0] // 2), jnp.bfloat16)
    return local_kernel(input_grad_kernel, out_shape, 2 * weight.size * grad.shape[0], (weight, grad))


def token_sum_kernel(place_ref, block_ref, grad_ref, total_ref):
    tokens = 2 * block_ref.shape[2]
    blocks = []
    for row in range(ROWS):
        parts = [block_ref[place_ref[2 * row + d]] for d in range(2)]
        blocks.append(jnp.concatenate(parts, axis=1))
    for start in range(0, total_ref.shape[1], LANES):
        units = pl.ds(start, LANES)
        total = None
        for row, block in enumerate(blocks):
            term = jnp.dot(
                block,
                grad_ref[pl.ds(row * tokens, tokens), units],
                preferred_element_type=jnp.float32,
            )
            total = term if total is None else total + term
        total_ref[:, units] = total.astype(total_ref.dtype)


def token_sum(place, blocks, grads):
    depth = blocks.shape[1]
    out_shape = jax.ShapeDtypeStruct((depth, grads.shape[1]), jnp.bfloat16)
    return local_kernel(
        token_sum_kernel, out_shape, 2 * depth * grads.size, (blocks, grads), place
    )


def places():
    tables = []
    for replica in range(2):
        for col in range(COLS):
            y, x = divmod(col, SIDE)
            tables.append(
                [
                    ((x - c) % SIDE * SIDE + (y - c // SIDE) % SIDE) * 2 + (replica ^ d)
                    for c in range(COLS)
                    for d in range(2)
                ]
            )
    return jnp.array(tables, jnp.int32)[lax.axis_index(("dp",) + COL)]


def shifted(value, axis, steps):
    return lax.ppermute(value, axis, [(i, (i + steps) % SIDE) for i in range(SIDE)])


def from_line(pair):
    return jnp.concatenate([pair] + [shifted(pair, "y", d) for d in range(1, SIDE)])


def turn_moves(other):
    moves = []
    for d in range(2):
        for r in range(ROWS):
            for c in range(COLS):
                source, target = ((d * ROWS + r) * COLS + c, ((d ^ other) * ROWS + c) * COLS + r)
                moves.append((source, target))
    return moves


def from_lines(line):
    return jnp.concatenate([line] + [shifted(line, "x", e) for e in range(1, SIDE)])


def to_replica(value):
    return lax.ppermute(value, "dp", [(0, 1), (1, 0)])


def to_all(block, axis, size):
    copies = jnp.broadcast_to(block[None], (size,) + block.shape)
    return lax.all_to_all(copies, axis, 0, 0, tiled=True)


def sum_along(pieces, axis):
    pieces = lax.all_to_all(pieces, axis, 0, 0, tiled=True)
    return jnp.sum(pieces.astype(jnp.float32), axis=0).astype(jnp.bfloat16)


def per_device(features, up_weight, out_grad):
    tokens, depth = features.shape
    half = up_weight.shape[1] // 2
    replica = lax.axis_index("dp")
    features = features.T

    def half_of(value, which):
        return lax.dynamic_slice_in_dim(value, which * half, half, axis=1)

    def by_replica(mine, other, axis):
        parts = jnp.where(replica == 0, mine, other), jnp.where(replica == 0, other, mine)
        return jnp.concatenate(parts, axis=axis)

    weight = lax.all_gather(half_of(up_weight, replica), "row", axis=0, tiled=True)
    turned = [lax.ppermute(features, ("dp", "row") + COL, turn_moves(other)) for other in (0, 1)]
    turned = jnp.stack(turned)
    depth_line = to_all(features, ("dp", "y"), 2 * SIDE)
    by_depth = to_all(depth_line, "x", SIDE)
    out_grad = by_replica(
        half_of(out_grad, replica), to_replica(half_of(out_grad, 1 - replica)), 0
    )

    hidden = hidden_sum(after(by_depth, turned), weight)
    normal_cdf = 0.5 * (1.0 + jax.scipy.special.erf(hidden / math.sqrt(2.0)))
    density = jnp.exp(-0.5 * hidden * hidden) / math.sqrt(2.0 * math.pi)
    gelu_half = (hidden * normal_cdf).astype(jnp.bfloat16)
    hidden_grad = (out_grad.astype(jnp.float32) * (normal_cdf + hidden * density)).astype(
        jnp.bfloat16
    )
    grads = lax.all_gather(hidden_grad, "row", axis=0, tiled=True)

    by_token = from_lines(from_line(after(turned, hidden_grad)))
    pieces = input_grad_pieces(weight, hidden_grad)
    own = token_sum(places(), by_token, grads)
    feature_grad = sum_along(sum_along(pieces, "x"), ("dp", "y")).T

    mine, other = (
        lax.dynamic_slice_in_dim(gelu_half, which * tokens, tokens, axis=0)
        for which in (replica, 1 - replica)
    )
    gelu_out = by_replica(mine, to_replica(other), 1)
    weight_grad = by_replica(own, to_replica(own), 1).astype(jnp.float32)
    return (gelu_out, feature_grad, weight_grad)


def solution(mesh):
    names = ("dp", "row") + COL
    fine = Mesh(mesh.devices.reshape(2, ROWS, SIDE, SIDE), names)
    by_tokens = P(("dp", "row"), COL)
    placed = (by_tokens, P("row", COL), by_tokens)
    return jax.shard_map(
        per_device,
        mesh=fine,
        in_specs=placed,
        out_specs=(by_tokens, by_tokens, P("row", COL)),
        check_vma=False,
    )
```

```python
import math

import jax
import jax.numpy as jnp
from jax import lax
from jax.experimental import pallas as pl
from jax.experimental.pallas import tpu as pltpu
from jax.sharding import Mesh
from jax.sharding import PartitionSpec as P

ROWS = 16
COLS = 16
SIDE = 4
LANES = 256
VMEM_BYTES = 32 * 2**20
COL = ("y", "x")


def after(value, *others):
    return lax.optimization_barrier((value,) + others)[0]


def local_kernel(kernel, out_shape, flops, operands, place=None):
    moved = sum(x.size * x.dtype.itemsize for x in (*operands, out_shape))
    in_specs = [pl.BlockSpec(memory_space=pltpu.VMEM)] * len(operands)
    if place is not None:
        in_specs = [pl.BlockSpec(memory_space=pltpu.SMEM)] + in_specs
        operands = (place, *operands)
    return pl.pallas_call(
        kernel,
        out_shape=out_shape,
        in_specs=in_specs,
        out_specs=pl.BlockSpec(memory_space=pltpu.VMEM),
        compiler_params=pltpu.CompilerParams(vmem_limit_bytes=VMEM_BYTES),
        cost_estimate=pl.CostEstimate(flops=flops, bytes_accessed=moved, transcendentals=0),
    )(*operands)


def both_replicas(block_ref, col):
    y, x = divmod(col, SIDE)
    return jnp.concatenate([block_ref[x, y], block_ref[x, SIDE + y]], axis=1)


def hidden_kernel(block_ref, weight_ref, hidden_ref):
    depth = block_ref.shape[2]
    blocks = [both_replicas(block_ref, col) for col in range(COLS)]
    for start in range(0, hidden_ref.shape[1], LANES):
        units = pl.ds(start, LANES)
        total = None
        for col, block in enumerate(blocks):
            term = lax.dot_general(
                block,
                weight_ref[pl.ds(col * depth, depth), units],
                (((0,), (0,)), ((), ())),
                preferred_element_type=jnp.float32,
            )
            total = term if total is None else total + term
        hidden_ref[:, units] = total


def hidden_sum(blocks, weight):
    tokens = 2 * blocks.shape[3]
    out_shape = jax.ShapeDtypeStruct((tokens, weight.shape[1]), jnp.float32)
    return local_kernel(hidden_kernel, out_shape, 2 * tokens * weight.size, (blocks, weight))


def input_grad_kernel(weight_ref, grad_ref, pieces_ref):
    depth, tokens = pieces_ref.shape[2:]
    for col in range(COLS):
        y, x = divmod(col, SIDE)
        piece = lax.dot_general(
            weight_ref[pl.ds(col * depth, depth), :],
            grad_ref[...],
            (((1,), (1,)), ((), ())),
            preferred_element_type=jnp.float32,
        ).astype(jnp.bfloat16)
        pieces_ref[x, y] = piece[:, :tokens]
        pieces_ref[x, SIDE + y] = piece[:, tokens:]


def input_grad_pieces(weight, grad):
    depth = weight.shape[0] // COLS
    out_shape = jax.ShapeDtypeStruct((SIDE, 2 * SIDE, depth, grad.shape[0] // 2), jnp.bfloat16)
    return local_kernel(input_grad_kernel, out_shape, 2 * weight.size * grad.shape[0], (weight, grad))


def token_sum_kernel(place_ref, block_ref, grad_ref, total_ref):
    tokens = 2 * block_ref.shape[2]
    blocks = []
    for row in range(ROWS):
        parts = [block_ref[place_ref[2 * row + d]] for d in range(2)]
        blocks.append(jnp.concatenate(parts, axis=1))
    for start in range(0, total_ref.shape[1], LANES):
        units = pl.ds(start, LANES)
        total = None
        for row, block in enumerate(blocks):
            term = jnp.dot(
                block,
                grad_ref[pl.ds(row * tokens, tokens), units],
                preferred_element_type=jnp.float32,
            )
            total = term if total is None else total + term
        total_ref[:, units] = total.astype(total_ref.dtype)


def token_sum(place, blocks, grads):
    depth = blocks.shape[1]
    out_shape = jax.ShapeDtypeStruct((depth, grads.shape[1]), jnp.bfloat16)
    return local_kernel(
        token_sum_kernel, out_shape, 2 * depth * grads.size, (blocks, grads), place
    )


def places():
    tables = []
    for replica in range(2):
        for col in range(COLS):
            y, x = divmod(col, SIDE)
            tables.append(
                [
                    ((x - c) % SIDE * SIDE + (y - c // SIDE) % SIDE) * 2 + (replica ^ d)
                    for c in range(COLS)
                    for d in range(2)
                ]
            )
    return jnp.array(tables, jnp.int32)[lax.axis_index(("dp",) + COL)]


def shifted(value, axis, steps):
    return lax.ppermute(value, axis, [(i, (i + steps) % SIDE) for i in range(SIDE)])


def from_line(pair):
    return jnp.concatenate([pair] + [shifted(pair, "y", d) for d in range(1, SIDE)])


def turn_moves(other):
    moves = []
    for d in range(2):
        for r in range(ROWS):
            for c in range(COLS):
                source, target = ((d * ROWS + r) * COLS + c, ((d ^ other) * ROWS + c) * COLS + r)
                moves.append((source, target))
    return moves


def from_lines(line):
    return jnp.concatenate([line] + [shifted(line, "x", e) for e in range(1, SIDE)])


def to_replica(value):
    return lax.ppermute(value, "dp", [(0, 1), (1, 0)])


def to_all(block, axis, size):
    copies = jnp.broadcast_to(block[None], (size,) + block.shape)
    return lax.all_to_all(copies, axis, 0, 0, tiled=True)


def sum_along(pieces, axis):
    pieces = lax.all_to_all(pieces, axis, 0, 0, tiled=True)
    return jnp.sum(pieces.astype(jnp.float32), axis=0).astype(jnp.bfloat16)


def per_device(features, up_weight, out_grad):
    tokens, depth = features.shape
    half = up_weight.shape[1] // 2
    replica = lax.axis_index("dp")
    features = features.T

    def half_of(value, which):
        return lax.dynamic_slice_in_dim(value, which * half, half, axis=1)

    def by_replica(mine, other, axis):
        parts = jnp.where(replica == 0, mine, other), jnp.where(replica == 0, other, mine)
        return jnp.concatenate(parts, axis=axis)

    weight = lax.all_gather(half_of(up_weight, replica), "row", axis=0, tiled=True)
    turned = [lax.ppermute(features, ("dp", "row") + COL, turn_moves(other)) for other in (0, 1)]
    turned = jnp.stack(turned)
    depth_line = to_all(after(features, turned), ("dp", "y"), 2 * SIDE)
    by_depth = to_all(depth_line, "x", SIDE)
    out_grad = by_replica(
        half_of(out_grad, replica), to_replica(half_of(out_grad, 1 - replica)), 0
    )

    hidden = hidden_sum(by_depth, weight)
    normal_cdf = 0.5 * (1.0 + jax.scipy.special.erf(hidden / math.sqrt(2.0)))
    density = jnp.exp(-0.5 * hidden * hidden) / math.sqrt(2.0 * math.pi)
    gelu_half = (hidden * normal_cdf).astype(jnp.bfloat16)
    hidden_grad = (out_grad.astype(jnp.float32) * (normal_cdf + hidden * density)).astype(
        jnp.bfloat16
    )
    grads = lax.all_gather(hidden_grad, "row", axis=0, tiled=True)

    by_token = from_lines(from_line(after(turned, hidden_grad)))
    pieces = input_grad_pieces(weight, hidden_grad)
    own = token_sum(places(), by_token, grads)
    feature_grad = sum_along(after(sum_along(pieces, "x"), own), ("dp", "y")).T

    mine, other = (
        lax.dynamic_slice_in_dim(gelu_half, which * tokens, tokens, axis=0)
        for which in (replica, 1 - replica)
    )
    gelu_out = by_replica(mine, to_replica(other), 1)
    weight_grad = by_replica(own, to_replica(own), 1).astype(jnp.float32)
    return (gelu_out, feature_grad, weight_grad)


def solution(mesh):
    names = ("dp", "row") + COL
    fine = Mesh(mesh.devices.reshape(2, ROWS, SIDE, SIDE), names)
    by_tokens = P(("dp", "row"), COL)
    placed = (by_tokens, P("row", COL), by_tokens)
    return jax.shard_map(
        per_device,
        mesh=fine,
        in_specs=placed,
        out_specs=(by_tokens, by_tokens, P("row", COL)),
        check_vma=False,
    )
```

```python
import math

import jax
import jax.numpy as jnp
from jax import lax
from jax.experimental import pallas as pl
from jax.experimental.pallas import tpu as pltpu
from jax.sharding import Mesh
from jax.sharding import PartitionSpec as P

ROWS = 16
COLS = 16
SIDE = 4
LANES = 256
VMEM_BYTES = 32 * 2**20
COL = ("y", "x")


def after(value, *others):
    return lax.optimization_barrier((value,) + others)[0]


def local_kernel(kernel, out_shape, flops, operands, place=None):
    moved = sum(x.size * x.dtype.itemsize for x in (*operands, out_shape))
    in_specs = [pl.BlockSpec(memory_space=pltpu.VMEM)] * len(operands)
    if place is not None:
        in_specs = [pl.BlockSpec(memory_space=pltpu.SMEM)] + in_specs
        operands = (place, *operands)
    return pl.pallas_call(
        kernel,
        out_shape=out_shape,
        in_specs=in_specs,
        out_specs=pl.BlockSpec(memory_space=pltpu.VMEM),
        compiler_params=pltpu.CompilerParams(vmem_limit_bytes=VMEM_BYTES),
        cost_estimate=pl.CostEstimate(flops=flops, bytes_accessed=moved, transcendentals=0),
    )(*operands)


def both_replicas(block_ref, col):
    y, x = divmod(col, SIDE)
    return jnp.concatenate([block_ref[x, y], block_ref[x, SIDE + y]], axis=1)


def hidden_kernel(block_ref, weight_ref, hidden_ref):
    depth = block_ref.shape[2]
    blocks = [both_replicas(block_ref, col) for col in range(COLS)]
    for start in range(0, hidden_ref.shape[1], LANES):
        units = pl.ds(start, LANES)
        total = None
        for col, block in enumerate(blocks):
            term = lax.dot_general(
                block,
                weight_ref[pl.ds(col * depth, depth), units],
                (((0,), (0,)), ((), ())),
                preferred_element_type=jnp.float32,
            )
            total = term if total is None else total + term
        hidden_ref[:, units] = total


def hidden_sum(blocks, weight):
    tokens = 2 * blocks.shape[3]
    out_shape = jax.ShapeDtypeStruct((tokens, weight.shape[1]), jnp.float32)
    return local_kernel(hidden_kernel, out_shape, 2 * tokens * weight.size, (blocks, weight))


def input_grad_kernel(weight_ref, grad_ref, pieces_ref):
    depth, tokens = pieces_ref.shape[2:]
    for col in range(COLS):
        y, x = divmod(col, SIDE)
        piece = lax.dot_general(
            weight_ref[pl.ds(col * depth, depth), :],
            grad_ref[...],
            (((1,), (1,)), ((), ())),
            preferred_element_type=jnp.float32,
        ).astype(jnp.bfloat16)
        pieces_ref[x, y] = piece[:, :tokens]
        pieces_ref[x, SIDE + y] = piece[:, tokens:]


def input_grad_pieces(weight, grad):
    depth = weight.shape[0] // COLS
    out_shape = jax.ShapeDtypeStruct((SIDE, 2 * SIDE, depth, grad.shape[0] // 2), jnp.bfloat16)
    return local_kernel(input_grad_kernel, out_shape, 2 * weight.size * grad.shape[0], (weight, grad))


def token_sum_kernel(place_ref, block_ref, grad_ref, total_ref):
    tokens = 2 * block_ref.shape[2]
    blocks = []
    for row in range(ROWS):
        parts = [block_ref[place_ref[2 * row + d]] for d in range(2)]
        blocks.append(jnp.concatenate(parts, axis=1))
    for start in range(0, total_ref.shape[1], LANES):
        units = pl.ds(start, LANES)
        total = None
        for row, block in enumerate(blocks):
            term = jnp.dot(
                block,
                grad_ref[pl.ds(row * tokens, tokens), units],
                preferred_element_type=jnp.float32,
            )
            total = term if total is None else total + term
        total_ref[:, units] = total.astype(total_ref.dtype)


def token_sum(place, blocks, grads):
    depth = blocks.shape[1]
    out_shape = jax.ShapeDtypeStruct((depth, grads.shape[1]), jnp.bfloat16)
    return local_kernel(
        token_sum_kernel, out_shape, 2 * depth * grads.size, (blocks, grads), place
    )


def places():
    tables = []
    for replica in range(2):
        for col in range(COLS):
            y, x = divmod(col, SIDE)
            tables.append(
                [
                    ((x - c) % SIDE * SIDE + (y - c // SIDE) % SIDE) * 2 + (replica ^ d)
                    for c in range(COLS)
                    for d in range(2)
                ]
            )
    return jnp.array(tables, jnp.int32)[lax.axis_index(("dp",) + COL)]


def shifted(value, axis, steps):
    return lax.ppermute(value, axis, [(i, (i + steps) % SIDE) for i in range(SIDE)])


def from_line(pair):
    return jnp.concatenate([pair] + [shifted(pair, "y", d) for d in range(1, SIDE)])


def turn_moves(other):
    moves = []
    for d in range(2):
        for r in range(ROWS):
            for c in range(COLS):
                source, target = ((d * ROWS + r) * COLS + c, ((d ^ other) * ROWS + c) * COLS + r)
                moves.append((source, target))
    return moves


def from_lines(line):
    return jnp.concatenate([line] + [shifted(line, "x", e) for e in range(1, SIDE)])


def to_replica(value):
    return lax.ppermute(value, "dp", [(0, 1), (1, 0)])


def to_all(block, axis, size):
    copies = jnp.broadcast_to(block[None], (size,) + block.shape)
    return lax.all_to_all(copies, axis, 0, 0, tiled=True)


def sum_along(pieces, axis):
    pieces = lax.all_to_all(pieces, axis, 0, 0, tiled=True)
    return jnp.sum(pieces.astype(jnp.float32), axis=0).astype(jnp.bfloat16)


def per_device(features, up_weight, out_grad):
    tokens, depth = features.shape
    half = up_weight.shape[1] // 2
    replica = lax.axis_index("dp")
    features = features.T

    def half_of(value, which):
        return lax.dynamic_slice_in_dim(value, which * half, half, axis=1)

    def by_replica(mine, other, axis):
        parts = jnp.where(replica == 0, mine, other), jnp.where(replica == 0, other, mine)
        return jnp.concatenate(parts, axis=axis)

    weight = lax.all_gather(half_of(up_weight, replica), "row", axis=0, tiled=True)
    turned = [lax.ppermute(features, ("dp", "row") + COL, turn_moves(other)) for other in (0, 1)]
    turned = jnp.stack(turned)
    depth_line = to_all(features, ("dp", "y"), 2 * SIDE)
    by_depth = to_all(depth_line, "x", SIDE)
    out_grad = by_replica(
        half_of(out_grad, replica), to_replica(half_of(out_grad, 1 - replica)), 0
    )

    hidden = hidden_sum(after(by_depth, turned), weight)
    normal_cdf = 0.5 * (1.0 + jax.scipy.special.erf(hidden / math.sqrt(2.0)))
    density = jnp.exp(-0.5 * hidden * hidden) / math.sqrt(2.0 * math.pi)
    gelu_half = (hidden * normal_cdf).astype(jnp.bfloat16)
    hidden_grad = (out_grad.astype(jnp.float32) * (normal_cdf + hidden * density)).astype(
        jnp.bfloat16
    )
    grads = lax.all_gather(hidden_grad, "row", axis=0, tiled=True)

    by_token = from_lines(from_line(after(turned, hidden_grad)))
    pieces = input_grad_pieces(weight, hidden_grad)
    own = token_sum(places(), by_token, grads)
    feature_grad = sum_along(after(sum_along(pieces, "x"), grads), ("dp", "y")).T

    mine, other = (
        lax.dynamic_slice_in_dim(gelu_half, which * tokens, tokens, axis=0)
        for which in (replica, 1 - replica)
    )
    gelu_out = by_replica(mine, to_replica(other), 1)
    weight_grad = by_replica(own, to_replica(own), 1).astype(jnp.float32)
    return (gelu_out, feature_grad, weight_grad)


def solution(mesh):
    names = ("dp", "row") + COL
    fine = Mesh(mesh.devices.reshape(2, ROWS, SIDE, SIDE), names)
    by_tokens = P(("dp", "row"), COL)
    placed = (by_tokens, P("row", COL), by_tokens)
    return jax.shard_map(
        per_device,
        mesh=fine,
        in_specs=placed,
        out_specs=(by_tokens, by_tokens, P("row", COL)),
        check_vma=False,
    )
```

```python
import math

import jax
import jax.numpy as jnp
from jax import lax
from jax.experimental import pallas as pl
from jax.experimental.pallas import tpu as pltpu
from jax.sharding import Mesh
from jax.sharding import PartitionSpec as P

ROWS = 16
COLS = 16
SIDE = 4
LANES = 256
VMEM_BYTES = 32 * 2**20
COL = ("y", "x")


def after(value, *others):
    return lax.optimization_barrier((value,) + others)[0]


def local_kernel(kernel, out_shape, flops, operands, place=None):
    moved = sum(x.size * x.dtype.itemsize for x in (*operands, out_shape))
    in_specs = [pl.BlockSpec(memory_space=pltpu.VMEM)] * len(operands)
    if place is not None:
        in_specs = [pl.BlockSpec(memory_space=pltpu.SMEM)] + in_specs
        operands = (place, *operands)
    return pl.pallas_call(
        kernel,
        out_shape=out_shape,
        in_specs=in_specs,
        out_specs=pl.BlockSpec(memory_space=pltpu.VMEM),
        compiler_params=pltpu.CompilerParams(vmem_limit_bytes=VMEM_BYTES),
        cost_estimate=pl.CostEstimate(flops=flops, bytes_accessed=moved, transcendentals=0),
    )(*operands)


def both_replicas(block_ref, col):
    y, x = divmod(col, SIDE)
    return jnp.concatenate([block_ref[x, y], block_ref[x, SIDE + y]], axis=1)


def hidden_kernel(block_ref, weight_ref, hidden_ref):
    depth = block_ref.shape[2]
    blocks = [both_replicas(block_ref, col) for col in range(COLS)]
    for start in range(0, hidden_ref.shape[1], LANES):
        units = pl.ds(start, LANES)
        total = None
        for col, block in enumerate(blocks):
            term = lax.dot_general(
                block,
                weight_ref[pl.ds(col * depth, depth), units],
                (((0,), (0,)), ((), ())),
                preferred_element_type=jnp.float32,
            )
            total = term if total is None else total + term
        hidden_ref[:, units] = total


def hidden_sum(blocks, weight):
    tokens = 2 * blocks.shape[3]
    out_shape = jax.ShapeDtypeStruct((tokens, weight.shape[1]), jnp.float32)
    return local_kernel(hidden_kernel, out_shape, 2 * tokens * weight.size, (blocks, weight))


def input_grad_kernel(weight_ref, grad_ref, pieces_ref):
    depth, tokens = pieces_ref.shape[2:]
    for col in range(COLS):
        y, x = divmod(col, SIDE)
        piece = lax.dot_general(
            weight_ref[pl.ds(col * depth, depth), :],
            grad_ref[...],
            (((1,), (1,)), ((), ())),
            preferred_element_type=jnp.float32,
        ).astype(jnp.bfloat16)
        pieces_ref[x, y] = piece[:, :tokens]
        pieces_ref[x, SIDE + y] = piece[:, tokens:]


def input_grad_pieces(weight, grad):
    depth = weight.shape[0] // COLS
    out_shape = jax.ShapeDtypeStruct((SIDE, 2 * SIDE, depth, grad.shape[0] // 2), jnp.bfloat16)
    return local_kernel(input_grad_kernel, out_shape, 2 * weight.size * grad.shape[0], (weight, grad))


def token_sum_kernel(place_ref, block_ref, grad_ref, total_ref):
    tokens = 2 * block_ref.shape[2]
    blocks = []
    for row in range(ROWS):
        parts = [block_ref[place_ref[2 * row + d]] for d in range(2)]
        blocks.append(jnp.concatenate(parts, axis=1))
    for start in range(0, total_ref.shape[1], LANES):
        units = pl.ds(start, LANES)
        total = None
        for row, block in enumerate(blocks):
            term = jnp.dot(
                block,
                grad_ref[pl.ds(row * tokens, tokens), units],
                preferred_element_type=jnp.float32,
            )
            total = term if total is None else total + term
        total_ref[:, units] = total.astype(total_ref.dtype)


def token_sum(place, blocks, grads):
    depth = blocks.shape[1]
    out_shape = jax.ShapeDtypeStruct((depth, grads.shape[1]), jnp.bfloat16)
    return local_kernel(
        token_sum_kernel, out_shape, 2 * depth * grads.size, (blocks, grads), place
    )


def places():
    tables = []
    for replica in range(2):
        for col in range(COLS):
            y, x = divmod(col, SIDE)
            tables.append(
                [
                    ((x - c) % SIDE * SIDE + (y - c // SIDE) % SIDE) * 2 + (replica ^ d)
                    for c in range(COLS)
                    for d in range(2)
                ]
            )
    return jnp.array(tables, jnp.int32)[lax.axis_index(("dp",) + COL)]


def shifted(value, axis, steps):
    return lax.ppermute(value, axis, [(i, (i + steps) % SIDE) for i in range(SIDE)])


def from_line(pair):
    return jnp.concatenate([pair] + [shifted(pair, "y", d) for d in range(1, SIDE)])


def turn_moves(other):
    moves = []
    for d in range(2):
        for r in range(ROWS):
            for c in range(COLS):
                source, target = ((d * ROWS + r) * COLS + c, ((d ^ other) * ROWS + c) * COLS + r)
                moves.append((source, target))
    return moves


def from_lines(line):
    return [line] + [shifted(line, "x", e) for e in range(1, SIDE)]


def to_replica(value):
    return lax.ppermute(value, "dp", [(0, 1), (1, 0)])


def to_all(block, axis, size):
    copies = jnp.broadcast_to(block[None], (size,) + block.shape)
    return lax.all_to_all(copies, axis, 0, 0, tiled=True)


def sum_along(pieces, axis):
    pieces = lax.all_to_all(pieces, axis, 0, 0, tiled=True)
    return jnp.sum(pieces.astype(jnp.float32), axis=0).astype(jnp.bfloat16)


def per_device(features, up_weight, out_grad):
    tokens, depth = features.shape
    half = up_weight.shape[1] // 2
    replica = lax.axis_index("dp")
    features = features.T

    def half_of(value, which):
        return lax.dynamic_slice_in_dim(value, which * half, half, axis=1)

    def by_replica(mine, other, axis):
        parts = jnp.where(replica == 0, mine, other), jnp.where(replica == 0, other, mine)
        return jnp.concatenate(parts, axis=axis)

    weight = lax.all_gather(half_of(up_weight, replica), "row", axis=0, tiled=True)
    turned = [lax.ppermute(features, ("dp", "row") + COL, turn_moves(other)) for other in (0, 1)]
    turned = jnp.stack(turned)
    depth_line = to_all(features, ("dp", "y"), 2 * SIDE)
    by_depth = to_all(depth_line, "x", SIDE)
    out_grad = by_replica(
        half_of(out_grad, replica), to_replica(half_of(out_grad, 1 - replica)), 0
    )

    hidden = hidden_sum(after(by_depth, turned), weight)
    normal_cdf = 0.5 * (1.0 + jax.scipy.special.erf(hidden / math.sqrt(2.0)))
    density = jnp.exp(-0.5 * hidden * hidden) / math.sqrt(2.0 * math.pi)
    gelu_half = (hidden * normal_cdf).astype(jnp.bfloat16)
    hidden_grad = (out_grad.astype(jnp.float32) * (normal_cdf + hidden * density)).astype(
        jnp.bfloat16
    )
    grads = lax.all_gather(hidden_grad, "row", axis=0, tiled=True)

    token_lines = from_lines(from_line(after(turned, hidden_grad)))
    pieces = sum_along(input_grad_pieces(weight, hidden_grad), "x")
    feature_grad = sum_along(after(pieces, token_lines[1]), ("dp", "y"))
    own = token_sum(places(), after(jnp.concatenate(token_lines), feature_grad), grads)
    feature_grad = feature_grad.T

    mine, other = (
        lax.dynamic_slice_in_dim(gelu_half, which * tokens, tokens, axis=0)
        for which in (replica, 1 - replica)
    )
    gelu_out = by_replica(mine, to_replica(other), 1)
    weight_grad = by_replica(own, to_replica(own), 1).astype(jnp.float32)
    return (gelu_out, feature_grad, weight_grad)


def solution(mesh):
    names = ("dp", "row") + COL
    fine = Mesh(mesh.devices.reshape(2, ROWS, SIDE, SIDE), names)
    by_tokens = P(("dp", "row"), COL)
    placed = (by_tokens, P("row", COL), by_tokens)
    return jax.shard_map(
        per_device,
        mesh=fine,
        in_specs=placed,
        out_specs=(by_tokens, by_tokens, P("row", COL)),
        check_vma=False,
    )
```

```python
import math

import jax
import jax.numpy as jnp
from jax import lax
from jax.experimental import pallas as pl
from jax.experimental.pallas import tpu as pltpu
from jax.sharding import Mesh
from jax.sharding import PartitionSpec as P

ROWS = 16
COLS = 16
SIDE = 4
LANES = 256
CHUNKS = 4
VMEM_BYTES = 32 * 2**20
CHUNKED_VMEM_BYTES = 48 * 2**20
COL = ("y", "x")


def after(value, *others):
    return lax.optimization_barrier((value,) + others)[0]


def local_kernel(kernel, out_shape, flops, operands, place=None):
    moved = sum(x.size * x.dtype.itemsize for x in (*operands, out_shape))
    in_specs = [pl.BlockSpec(memory_space=pltpu.VMEM)] * len(operands)
    if place is not None:
        in_specs = [pl.BlockSpec(memory_space=pltpu.SMEM)] + in_specs
        operands = (place, *operands)
    return pl.pallas_call(
        kernel,
        out_shape=out_shape,
        in_specs=in_specs,
        out_specs=pl.BlockSpec(memory_space=pltpu.VMEM),
        compiler_params=pltpu.CompilerParams(vmem_limit_bytes=VMEM_BYTES),
        cost_estimate=pl.CostEstimate(flops=flops, bytes_accessed=moved, transcendentals=0),
    )(*operands)


def both_replicas(block_ref, col):
    y, x = divmod(col, SIDE)
    return jnp.concatenate([block_ref[x, y], block_ref[x, SIDE + y]], axis=1)


def chunk_copies(source_ref, held_ref, sems):
    rows = source_ref.shape[0] // CHUNKS
    copies = []
    for chunk in range(CHUNKS):
        span = pl.ds(chunk * rows, rows)
        copies.append(pltpu.make_async_copy(source_ref.at[span], held_ref.at[span], sems.at[chunk]))
    for copy in copies:
        copy.start()
    return copies


def chunked_sum(copies, count, term_of, total_ref):
    per_chunk = count // CHUNKS
    for chunk, copy in enumerate(copies):
        copy.wait()
        for start in range(0, total_ref.shape[1], LANES):
            units = pl.ds(start, LANES)
            total = total_ref[:, units] if chunk else None
            for index in range(chunk * per_chunk, (chunk + 1) * per_chunk):
                term = term_of(index, units)
                total = term if total is None else total + term
            total_ref[:, units] = total


def chunked_kernel(kernel, out_shape, flops, place, blocks, value, scratch=()):
    operands = ([] if place is None else [place]) + [blocks, value]
    vmem = pl.BlockSpec(memory_space=pltpu.VMEM)
    in_specs = [vmem, pl.BlockSpec(memory_space=pl.ANY)]
    if place is not None:
        in_specs = [pl.BlockSpec(memory_space=pltpu.SMEM)] + in_specs
    moved = sum(x.size * x.dtype.itemsize for x in (blocks, value, out_shape))
    return pl.pallas_call(
        kernel,
        out_shape=out_shape,
        in_specs=in_specs,
        out_specs=vmem,
        scratch_shapes=[
            pltpu.VMEM(value.shape, value.dtype),
            pltpu.SemaphoreType.DMA((CHUNKS,)),
            *scratch,
        ],
        compiler_params=pltpu.CompilerParams(vmem_limit_bytes=CHUNKED_VMEM_BYTES),
        cost_estimate=pl.CostEstimate(flops=flops, bytes_accessed=moved, transcendentals=0),
    )(*operands)


def hidden_kernel(block_ref, weight_ref, hidden_ref, held_ref, sems):
    depth = block_ref.shape[2]
    copies = chunk_copies(weight_ref, held_ref, sems)
    blocks = [both_replicas(block_ref, col) for col in range(COLS)]

    def term_of(col, units):
        return lax.dot_general(
            blocks[col],
            held_ref[pl.ds(col * depth, depth), units],
            (((0,), (0,)), ((), ())),
            preferred_element_type=jnp.float32,
        )

    chunked_sum(copies, COLS, term_of, hidden_ref)


def hidden_sum(blocks, weight):
    tokens = 2 * blocks.shape[3]
    out_shape = jax.ShapeDtypeStruct((tokens, weight.shape[1]), jnp.float32)
    return chunked_kernel(hidden_kernel, out_shape, 2 * tokens * weight.size, None, blocks, weight)


def input_grad_kernel(weight_ref, grad_ref, pieces_ref):
    depth, tokens = pieces_ref.shape[2:]
    for col in range(COLS):
        y, x = divmod(col, SIDE)
        piece = lax.dot_general(
            weight_ref[pl.ds(col * depth, depth), :],
            grad_ref[...],
            (((1,), (1,)), ((), ())),
            preferred_element_type=jnp.float32,
        ).astype(jnp.bfloat16)
        pieces_ref[x, y] = piece[:, :tokens]
        pieces_ref[x, SIDE + y] = piece[:, tokens:]


def input_grad_pieces(weight, grad):
    depth = weight.shape[0] // COLS
    out_shape = jax.ShapeDtypeStruct((SIDE, 2 * SIDE, depth, grad.shape[0] // 2), jnp.bfloat16)
    return local_kernel(input_grad_kernel, out_shape, 2 * weight.size * grad.shape[0], (weight, grad))


def token_sum_kernel(place_ref, block_ref, grad_ref, out_ref, held_ref, sems, total_ref):
    tokens = 2 * block_ref.shape[2]
    copies = chunk_copies(grad_ref, held_ref, sems)
    blocks = []
    for row in range(ROWS):
        parts = [block_ref[place_ref[2 * row + d]] for d in range(2)]
        blocks.append(jnp.concatenate(parts, axis=1))

    def term_of(row, units):
        grad = held_ref[pl.ds(row * tokens, tokens), units]
        return jnp.dot(blocks[row], grad, preferred_element_type=jnp.float32)

    chunked_sum(copies, ROWS, term_of, total_ref)
    out_ref[...] = total_ref[...].astype(out_ref.dtype)


def token_sum(place, blocks, grads):
    shape = (blocks.shape[1], grads.shape[1])
    out_shape = jax.ShapeDtypeStruct(shape, jnp.bfloat16)
    total = pltpu.VMEM(shape, jnp.float32)
    flops = 2 * shape[0] * grads.size
    return chunked_kernel(token_sum_kernel, out_shape, flops, place, blocks, grads, (total,))


def places():
    tables = []
    for replica in range(2):
        for col in range(COLS):
            y, x = divmod(col, SIDE)
            tables.append(
                [
                    ((x - c) % SIDE * SIDE + (y - c // SIDE) % SIDE) * 2 + (replica ^ d)
                    for c in range(COLS)
                    for d in range(2)
                ]
            )
    return jnp.array(tables, jnp.int32)[lax.axis_index(("dp",) + COL)]


def shifted(value, axis, steps):
    return lax.ppermute(value, axis, [(i, (i + steps) % SIDE) for i in range(SIDE)])


def from_line(block):
    pair = jnp.stack([block, to_replica(block)])
    return jnp.concatenate([pair] + [shifted(pair, "y", d) for d in range(1, SIDE)])


def from_lines(line):
    return jnp.concatenate([line] + [shifted(line, "x", e) for e in range(1, SIDE)])


def to_replica(value):
    return lax.ppermute(value, "dp", [(0, 1), (1, 0)])


def to_all(block, axis, size):
    copies = jnp.broadcast_to(block[None], (size,) + block.shape)
    return lax.all_to_all(copies, axis, 0, 0, tiled=True)


def sum_along(pieces, axis):
    pieces = lax.all_to_all(pieces, axis, 0, 0, tiled=True)
    return jnp.sum(pieces.astype(jnp.float32), axis=0).astype(jnp.bfloat16)


def per_device(features, up_weight, out_grad):
    tokens, depth = features.shape
    half = up_weight.shape[1] // 2
    replica = lax.axis_index("dp")
    features = features.T

    def half_of(value, which):
        return lax.dynamic_slice_in_dim(value, which * half, half, axis=1)

    def by_replica(mine, other, axis):
        parts = jnp.where(replica == 0, mine, other), jnp.where(replica == 0, other, mine)
        return jnp.concatenate(parts, axis=axis)

    weight = lax.all_gather(half_of(up_weight, replica), "row", axis=0, tiled=True)
    turns = [(r * COLS + c, c * COLS + r) for r in range(ROWS) for c in range(COLS)]
    turned = lax.ppermute(features, ("row",) + COL, turns)
    depth_line = to_all(features, ("dp", "y"), 2 * SIDE)
    by_depth = to_all(depth_line, "x", SIDE)
    out_grad = by_replica(
        half_of(out_grad, replica), to_replica(half_of(out_grad, 1 - replica)), 0
    )

    hidden = hidden_sum(after(by_depth, turned), weight)
    normal_cdf = 0.5 * (1.0 + jax.scipy.special.erf(hidden / math.sqrt(2.0)))
    density = jnp.exp(-0.5 * hidden * hidden) / math.sqrt(2.0 * math.pi)
    gelu_half = (hidden * normal_cdf).astype(jnp.bfloat16)
    hidden_grad = (out_grad.astype(jnp.float32) * (normal_cdf + hidden * density)).astype(
        jnp.bfloat16
    )
    grads = lax.all_gather(hidden_grad, "row", axis=0, tiled=True)

    by_token = from_lines(from_line(after(turned, hidden_grad)))
    pieces = input_grad_pieces(weight, hidden_grad)
    own = token_sum(places(), by_token, grads)
    feature_grad = sum_along(sum_along(pieces, "x"), ("dp", "y")).T

    mine, other = (
        lax.dynamic_slice_in_dim(gelu_half, which * tokens, tokens, axis=0)
        for which in (replica, 1 - replica)
    )
    gelu_out = by_replica(mine, to_replica(other), 1)
    weight_grad = by_replica(own, to_replica(own), 1).astype(jnp.float32)
    return (gelu_out, feature_grad, weight_grad)


def solution(mesh):
    names = ("dp", "row") + COL
    fine = Mesh(mesh.devices.reshape(2, ROWS, SIDE, SIDE), names)
    by_tokens = P(("dp", "row"), COL)
    placed = (by_tokens, P("row", COL), by_tokens)
    return jax.shard_map(
        per_device,
        mesh=fine,
        in_specs=placed,
        out_specs=(by_tokens, by_tokens, P("row", COL)),
        check_vma=False,
    )
```
